512 devices in a mesh: cam: 8 (over y_hi, core), frame: 64 (over x, y_lo, z).
Axes of the slice: x: 4, y: 8 (y_hi: 4, y_lo: 2; y = y_hi * 2 + y_lo), z: 8, core: 2. Of those that a mesh axis runs over, the one named last changes fastest.
Arguments:
- qkv: bfloat16 [3, 8, 64, 128, 1152], P(None, 'cam', 'frame'), may hold values from -20 to 20
- cross_q: bfloat16 [8, 64, 128, 1152], P('cam', 'frame'), may hold values from -20 to 20
- box_kv: bfloat16 [2, 64, 64, 1152], P(None, 'frame', 'cam'), may hold values from -20 to 20
- null_kv: bfloat16 [2, 1152], replicated, may hold values from -20 to 20
- view_link: int32 [8, 2], P('cam'), may hold values 0 or 1
- box_counts: int32 [64], P('frame'), may hold values from 1 to 64, 2048 in all
- box_visible: int32 [8, 64, 64], P('cam', 'frame'), may hold values 0 or 1
Outputs:
- blended: bfloat16 [8, 64, 128, 1152], P('cam', 'frame')
The draws below stay inside these ranges and needn't reach their ends.
Inputs may be any that keep to these rules, and one draw needn't show every extreme that they name: `box_counts`: some frame has all 64 slots filled.
All inputs are finite; a program needn't handle non-finite values. No bound on the sum of `view_link` or of `box_counts` or of `box_visible` on one device may be relied on, other than what follows from the above.
Results may differ from the reference program's by a relative error of at most 0.0045.
Values may be sent and summed in bfloat16 or wider, within the bound.
A program may use at most 64 MiB of HBM per device.

```python
import math
import jax
import jax.numpy as jnp
import numpy as np
from jax import lax

D = 1152
HEADS = 16
P_SIZE = 128
NBOX = 64
CAM = 8
FRAMES = 64
CLIP_LEN = 32
CLIPS = 2


def draw_qkv(key, part):
    key = jax.random.fold_in(key, 11)
    key_one = jax.random.fold_in(key, 0)
    array_shape = (3, CAM, FRAMES, P_SIZE, D)
    values = jnp.clip(jax.random.normal(key_one, array_shape, jnp.float32), -6.0, 6.0)
    return jnp.clip(values, -20.0, 20.0).astype(jnp.bfloat16)


def draw_cross_q(key, part):
    key = jax.random.fold_in(key, 12)
    key_one = jax.random.fold_in(key, 0)
    array_shape = (CAM, FRAMES, P_SIZE, D)
    values = jnp.clip(jax.random.normal(key_one, array_shape, jnp.float32), -6.0, 6.0)
    return jnp.clip(values, -20.0, 20.0).astype(jnp.bfloat16)


def draw_null_kv(key, part):
    key = jax.random.fold_in(key, 13)
    values = jnp.clip(jax.random.normal(key, (2, D), jnp.float32), -6.0, 6.0)
    return jnp.clip(values, -20.0, 20.0).astype(jnp.bfloat16)


def draw_box_kv(key, part):
    key = jax.random.fold_in(key, 14)
    key_one = jax.random.fold_in(key, 0)
    array_shape = (2, FRAMES, NBOX, D)
    values = jnp.clip(jax.random.normal(key_one, array_shape, jnp.float32), -6.0, 6.0)
    return jnp.clip(values, -20.0, 20.0).astype(jnp.bfloat16)


def plant(values, stream_key, low, top_value):
    extent = values.shape
    spot = [jax.random.randint(jax.random.fold_in(stream_key, axis), (), 0, extent[axis]) for axis in range(len(extent))]
    values = values.at[tuple(spot)].set(low)
    longest = extent.index(max(extent))
    spot[longest] = (spot[longest] + 1) % extent[longest]
    return values.at[tuple(spot)].set(top_value)


def length_profile(count, total, most, slope):
    loads = [(1 << 20) // math.isqrt(grade ** slope) + 1 for grade in range(2, count + 1)]
    spare, holding = total - most - (count - 1), [1] * (count - 1)
    while spare > 0:
        movable = [i for i in range(count - 1) if holding[i] < most]
        whole, remaining = sum([loads[i] for i in movable]), spare
        for i in movable:
            addition = min(most - holding[i], max(1, remaining * loads[i] // whole), spare)
            holding[i] = holding[i] + addition
            spare = spare - addition
    return np.array([most] + holding)


def uneven_parts(rng, number_of, total, limit, slope):
    if number_of == 2:
        one = jax.random.randint(rng, (), max(1, total - limit), min(limit, total - 1) + 1)
        return jnp.stack([one, total - one])
    sizes = jnp.asarray(length_profile(number_of, total, limit, slope), jnp.int32)
    twos = (number_of - 1) // 2
    donor, receiver = sizes[1:1 + 2 * twos:2], sizes[2:2 + 2 * twos:2]
    room = jnp.minimum(donor - 1, limit - receiver)
    shifted = jax.random.randint(jax.random.fold_in(rng, 1), (twos,), 0, 1 << 20) % (room + 1)
    sizes = sizes.at[1:1 + 2 * twos:2].set(donor - shifted).at[2:2 + 2 * twos:2].set(receiver + shifted)
    return sizes[jax.random.permutation(jax.random.fold_in(rng, 2), number_of)]


def setup_inputs(seed: int = 0) -> dict:
    splits = jax.random.split(jax.random.key(seed), 8)
    return {
        "qkv": draw_qkv(jax.random.fold_in(splits[7], 71), 0),
        "cross_q": draw_cross_q(jax.random.fold_in(splits[7], 71), 0),
        "box_kv": draw_box_kv(jax.random.fold_in(splits[7], 71), 0),
        "null_kv": draw_null_kv(jax.random.fold_in(splits[7], 71), 0),
        "view_link": plant((jax.random.randint(splits[4], (CAM, 2), 0, 4) < 3).astype(jnp.int32), jax.random.fold_in(splits[4], 1), 0, 1),
        "box_counts": uneven_parts(splits[5], FRAMES, FRAMES * NBOX // 2, NBOX, 1).astype(jnp.int32),
        "box_visible": plant((jax.random.randint(splits[6], (CAM, FRAMES, NBOX), 0, 4) < 3).astype(jnp.int32), jax.random.fold_in(splits[6], 1), 0, 1),
    }


def attend(query_rows, key_rows, value_rows, usable):
    row_count = query_rows.shape[0]
    feature_width = query_rows.shape[1]
    head_dim = feature_width // HEADS
    query_heads = query_rows.astype(jnp.float32).reshape(row_count, HEADS, head_dim)
    key_heads = key_rows.astype(jnp.float32).reshape(key_rows.shape[0], HEADS, head_dim)
    value_heads = value_rows.astype(jnp.float32).reshape(value_rows.shape[0], HEADS, head_dim)
    scores = jnp.einsum('rhd,khd->hrk', query_heads, key_heads) * (1.0 / math.sqrt(head_dim))
    scores = jnp.where(usable[None, None, :], scores, -jnp.inf)
    row_max = lax.optimization_barrier(jnp.max(scores, axis=2, keepdims=True))
    weights = jnp.exp(scores - row_max)
    weight_sum = lax.optimization_barrier(jnp.sum(weights, axis=2))
    packed = lax.optimization_barrier(weights.astype(jnp.bfloat16)).astype(jnp.float32)
    combined = jnp.einsum('hrk,khd->rhd', packed, value_heads)
    return (combined / weight_sum.T[:, :, None]).reshape(row_count, feature_width)

def clip_attention(stacked):
    query_rows = stacked[0].astype(jnp.float32)
    key_rows = stacked[1].astype(jnp.float32)
    value_rows = stacked[2].astype(jnp.float32)
    frame_count, item_count, feature_width = query_rows.shape
    head_dim = feature_width // HEADS
    query_heads = query_rows.reshape(frame_count, item_count, HEADS, head_dim)
    key_heads = key_rows.reshape(frame_count, item_count, HEADS, head_dim)
    value_heads = value_rows.reshape(frame_count, item_count, HEADS, head_dim)
    scores = jnp.einsum('fihd,gihd->ihfg', query_heads, key_heads) * (1.0 / math.sqrt(head_dim))
    row_max = lax.optimization_barrier(jnp.max(scores, axis=3, keepdims=True))
    weights = jnp.exp(scores - row_max)
    weight_sum = lax.optimization_barrier(jnp.sum(weights, axis=3))
    packed = lax.optimization_barrier(weights.astype(jnp.bfloat16)).astype(jnp.float32)
    combined = jnp.einsum('ihfg,gihd->fihd', packed, value_heads)
    result = combined / jnp.transpose(weight_sum, (2, 0, 1))[..., None]
    return result.reshape(frame_count, item_count, feature_width)

def frame_attention(stacked):
    pieces = []
    for clip_id in range(CLIPS):
        start = clip_id * CLIP_LEN
        pieces.append(clip_attention(stacked[:, start:start + CLIP_LEN]))
    return jnp.concatenate(pieces, 0)

def reference(qkv, cross_q, box_kv, null_kv, view_link, box_counts, box_visible):
    slot_ids = jnp.arange(NBOX, dtype=jnp.int32)

    def camera_block(camera):
        left_cam = (camera + CAM - 1) % CAM
        right_cam = (camera + 1) % CAM

        def frame_block(frame_id):
            query_rows = qkv[0, camera, frame_id]
            key_rows = jnp.concatenate([qkv[1, camera, frame_id], qkv[1, left_cam, frame_id], qkv[1, right_cam, frame_id]], 0)
            value_rows = jnp.concatenate([qkv[2, camera, frame_id], qkv[2, left_cam, frame_id], qkv[2, right_cam, frame_id]], 0)
            usable = jnp.concatenate([jnp.ones((P_SIZE,), jnp.bool_), jnp.broadcast_to(view_link[camera, 0] == 1, (P_SIZE,)), jnp.broadcast_to(view_link[camera, 1] == 1, (P_SIZE,))])
            view_out = attend(query_rows, key_rows, value_rows, usable)
            box_keys = jnp.concatenate([null_kv[0:1], box_kv[0, frame_id]], 0)
            box_values = jnp.concatenate([null_kv[1:2], box_kv[1, frame_id]], 0)
            live_slots = (slot_ids < box_counts[frame_id]) & (box_visible[camera, frame_id] == 1)
            box_usable = jnp.concatenate([jnp.ones((1,), jnp.bool_), live_slots])
            cross_out = attend(cross_q[camera, frame_id], box_keys, box_values, box_usable)
            return view_out + cross_out
        spatial = lax.map(frame_block, jnp.arange(FRAMES, dtype=jnp.int32))
        time_out = frame_attention(qkv[:, camera])
        time_out = lax.optimization_barrier(time_out.astype(jnp.bfloat16)).astype(jnp.float32)
        return (spatial + time_out).astype(jnp.bfloat16)
    return lax.map(camera_block, jnp.arange(CAM, dtype=jnp.int32))
```

```python
import functools
import math

import jax
import jax.numpy as jnp
from jax import lax
from jax.experimental import pallas as pl
from jax.experimental.pallas import tpu as pltpu
from jax.sharding import PartitionSpec as P

MESH = pl.DeviceIdType.MESH
HEADS = 16
ROWS = 128
WIDTH = 1152
HEAD_DIM = WIDTH // HEADS
TILE = 128
SCALE = 1.0 / math.sqrt(HEAD_DIM)
FAR = -1e30
BF16 = jnp.bfloat16
F32 = jnp.float32
PARTS = ((0, 3), (3, 6), (6, 9))


def head_window(head):
    low = head * HEAD_DIM
    first = low // TILE
    last = (low + HEAD_DIM - 1) // TILE
    return low, first, last + 1


def heads_and_tiles():
    plan = []
    head_done = tile_done = 0
    for _, high in PARTS:
        heads = (high * TILE) // HEAD_DIM
        tiles = WIDTH // TILE if heads == HEADS else (heads * HEAD_DIM) // TILE
        plan.append((range(head_done, heads), (tile_done, tiles)))
        head_done, tile_done = heads, tiles
    return plan


def cols(first, last):
    return pl.ds(first * TILE, (last - first) * TILE)


def attend_heads(heads, q_ref, k_ref, v_ref, bias, emit, tiles):
    for head in heads:
        low, first, last = head_window(head)
        span = (last - first) * TILE
        lane = lax.broadcasted_iota(jnp.int32, (1, span), 1) + first * TILE
        mine = (lane >= low) & (lane < low + HEAD_DIM)
        window = pl.ds(first * TILE, span)
        q = q_ref[:, window] * mine.astype(F32).astype(BF16)
        scores = lax.dot_general(
            q, k_ref[:, window], (((1,), (1,)), ((), ())), preferred_element_type=F32
        )
        scores = scores + bias
        top = jnp.max(scores, axis=1, keepdims=True)
        weights = jnp.exp((scores - top) * SCALE)
        total = jnp.sum(weights, axis=1, keepdims=True)
        result = jnp.dot(weights.astype(BF16), v_ref[:, window], preferred_element_type=F32)
        result = result * (1.0 / total)
        for tile in range(first, last):
            at = (tile - first) * TILE
            part = result[:, at : at + TILE]
            if tile in tiles:
                part = jnp.where(mine[:, at : at + TILE], part, tiles[tile])
            tiles[tile] = part
            if low + HEAD_DIM >= (tile + 1) * TILE:
                emit(tile, tiles.pop(tile))


def kernel(
    qkv, cross_q, box_kv, null_kv, view_link, box_counts, box_visible, out,
    q_own, kv_all, z_in, z_perm, home, t_out, t_in, t_perm, t_fin,
    cq, boxes, nulls, ckv, vl, bc, bv, bv_wide, acc,
    local_sem, z_send, z_recv, xy_send, xy_recv, rxy_send, rxy_recv, rz_send, rz_recv,
    view_send, view_recv, box_send, box_recv, pair_send, pair_recv, own_sem,
):
    cam = lax.axis_index("cam")
    frame = lax.axis_index("frame")
    x, y, z = frame // 16, (frame // 8) % 2, frame % 8
    half = x % 2
    spot = half * 2 + y

    def z_peer(d):
        return (cam, x * 16 + y * 8 + (z + d) % 8)

    def spot_of(dx, dy):
        return ((half + dx) % 2) * 2 + (y + dy) % 2

    def xy_peer(dx, dy):
        return (cam, ((x // 2) * 2 + (half + dx) % 2) * 16 + ((y + dy) % 2) * 8 + z)

    def cam_peer(d):
        return ((cam + d) % 8, frame)

    pair = ((cam // 2) * 2 + (cam + 1) % 2, frame)
    z_order = (1, 7, 2, 6, 3, 5, 4)
    xy_order = ((0, 1), (1, 0), (1, 1))

    barrier = pltpu.get_barrier_semaphore()
    peers = [z_peer(d) for d in z_order] + [xy_peer(*d) for d in xy_order]
    peers += [cam_peer(d) for d in (1, 7, 2, 6, 4)]
    for peer in peers:
        pl.semaphore_signal(barrier, inc=1, device_id=peer, device_id_type=MESH)

    def rows16(i):
        return pl.ds(pl.multiple_of(i * 16, 16), 16)

    def rows32(i):
        return pl.ds(pl.multiple_of(i * 32, 32), 32)

    local = []
    for src, dst in (
        (box_kv, boxes.at[cam]),
        (null_kv, nulls),
        (view_link, vl),
        (box_counts, bc),
        (box_visible, bv),
        (cross_q, cq),
        (qkv.at[:, rows16(z)], z_in.at[:, rows16(z)]),
        (qkv.at[0], q_own),
        (qkv.at[pl.ds(1, 2)], kv_all.at[:, pl.ds(0, ROWS)]),
    ):
        copy = pltpu.make_async_copy(src, dst, local_sem.at[len(local)])
        copy.start()
        local.append(copy)

    pl.semaphore_wait(barrier, len(peers))

    def remote(src, dst, send, recv, peer):
        copy = pltpu.make_async_remote_copy(
            src_ref=src, dst_ref=dst, send_sem=send, recv_sem=recv, device_id=peer,
            device_id_type=MESH,
        )
        copy.start()
        return copy

    sent = []

    def send_z(part):
        first, last = PARTS[part]
        copies = []
        for i, d in enumerate(z_order):
            copies.append(
                remote(
                    qkv.at[:, rows16((z + d) % 8), cols(first, last)],
                    z_in.at[:, rows16(z), cols(first, last)],
                    z_send.at[part, i], z_recv.at[part, i], z_peer(d),
                )
            )
        sent.extend(copies)
        return copies

    z_copies = [send_z(0)]
    box_copies = []
    for i, d in enumerate((2, 6, 4)):
        box_copies.append(
            remote(box_kv, boxes.at[cam], box_send.at[i], box_recv.at[i], cam_peer(d))
        )
    pair_copies = [remote(box_kv, boxes.at[cam], pair_send.at[0], pair_recv.at[0], pair)]
    view_copies = []
    for i, d in enumerate((1, 7)):
        view_copies.append(
            remote(
                qkv.at[pl.ds(1, 2)], kv_all.at[:, pl.ds(ROWS * (i + 1), ROWS)],
                view_send.at[i], view_recv.at[i], cam_peer(d),
            )
        )
    z_copies.append(send_z(1))
    z_copies.append(send_z(2))

    for i, d in enumerate((2, 6, 4)):
        box_copies[i].wait_recv()
        block = boxes.at[(cam + 8 - d) % 8]
        pair_copies.append(
            remote(block, block, pair_send.at[i + 1], pair_recv.at[i + 1], pair)
        )

    row = lax.broadcasted_iota(jnp.int32, (ROWS, ROWS), 0)
    col = lax.broadcasted_iota(jnp.int32, (ROWS, ROWS), 1)

    def by_group(r):
        return ((r >> 2) & 7) * 16 + (r >> 5) * 4 + (r & 3)

    to_group = (col == by_group(row)).astype(F32).astype(BF16)
    to_frame = (row == by_group(col)).astype(F32).astype(BF16)
    same_patch = jnp.where(((row ^ col) & 3) == 0, 0.0, FAR).astype(F32)

    for copy in local:
        copy.wait()
    for copy in pair_copies:
        copy.wait_recv()

    ckv[...] = jnp.zeros_like(ckv)
    for t in range(2):
        slots = jnp.concatenate([boxes[c, t].astype(F32) for c in range(8)], axis=0)
        ckv[t, 0:64, :] = slots.astype(BF16)
        first_row = lax.broadcasted_iota(jnp.int32, (16, WIDTH), 0) == 0
        null_row = jnp.broadcast_to(nulls[t : t + 1, :].astype(F32), (16, WIDTH))
        ckv[t, 64:80, :] = jnp.where(first_row, null_row, 0.0).astype(BF16)
    bv_wide[...] = jnp.zeros_like(bv_wide)
    bv_wide[:, 0:64] = bv[...]
    lane = lax.broadcasted_iota(jnp.int32, (1, ROWS), 1)
    live = ((lane < bc[...]) & (bv_wide[...] == 1)) | (lane == 64)
    cross_bias = jnp.where(live, 0.0, FAR).astype(F32)

    def emit_cross(tile, value):
        acc[:, cols(tile, tile + 1)] = value

    attend_heads(range(HEADS), cq, ckv.at[0], ckv.at[1], cross_bias, emit_cross, {})

    plan = heads_and_tiles()

    def permute_in(part):
        for copy in z_copies[part]:
            copy.wait_recv()
        first, last = PARTS[part]
        for t in range(3):
            moved = jnp.dot(to_group, z_in[t, :, cols(first, last)], preferred_element_type=F32)
            z_perm[t, :, cols(first, last)] = moved.astype(BF16)
        copies = []
        for i, d in enumerate(xy_order):
            copies.append(
                remote(
                    z_perm.at[:, rows32(spot_of(*d)), cols(first, last)],
                    home.at[:, rows32(spot), cols(first, last)],
                    xy_send.at[part, i], xy_recv.at[part, i], xy_peer(*d),
                )
            )
        own = pltpu.make_async_copy(
            z_perm.at[:, rows32(spot), cols(first, last)],
            home.at[:, rows32(spot), cols(first, last)],
            own_sem.at[0, part],
        )
        own.start()
        sent.extend(copies)
        return copies, own

    half_tiles = {}

    def emit_time(tile, value):
        t_out[:, cols(tile, tile + 1)] = value.astype(BF16)

    def time_heads(part, arriving):
        copies, own = arriving
        for copy in copies:
            copy.wait_recv()
        own.wait()
        heads, (first, last) = plan[part]
        attend_heads(heads, home.at[0], home.at[1], home.at[2], same_patch, emit_time, half_tiles)
        back = []
        for i, d in enumerate(xy_order):
            back.append(
                remote(
                    t_out.at[rows32(spot_of(*d)), cols(first, last)],
                    t_in.at[rows32(spot), cols(first, last)],
                    rxy_send.at[part, i], rxy_recv.at[part, i], xy_peer(*d),
                )
            )
        mine = pltpu.make_async_copy(
            t_out.at[rows32(spot), cols(first, last)],
            t_in.at[rows32(spot), cols(first, last)],
            own_sem.at[1, part],
        )
        mine.start()
        sent.extend(back)
        return back, mine

    def permute_back(part, arriving):
        copies, own = arriving
        for copy in copies:
            copy.wait_recv()
        own.wait()
        _, (first, last) = plan[part]
        moved = jnp.dot(to_frame, t_in[:, cols(first, last)], preferred_element_type=F32)
        t_perm[:, cols(first, last)] = moved.astype(BF16)
        back = []
        for i, d in enumerate(z_order):
            back.append(
                remote(
                    t_perm.at[rows16((z + d) % 8), cols(first, last)],
                    t_fin.at[rows16(z), cols(first, last)],
                    rz_send.at[part, i], rz_recv.at[part, i], z_peer(d),
                )
            )
        mine = pltpu.make_async_copy(
            t_perm.at[rows16(z), cols(first, last)],
            t_fin.at[rows16(z), cols(first, last)],
            own_sem.at[2, part],
        )
        mine.start()
        sent.extend(back)
        return back, mine

    def finish(part, arriving):
        copies, own = arriving
        for copy in copies:
            copy.wait_recv()
        own.wait()
        _, (first, last) = plan[part]
        at = cols(first, last)
        out[:, at] = (acc[:, at] + t_fin[:, at].astype(F32)).astype(BF16)

    def emit_view(tile, value):
        at = cols(tile, tile + 1)
        acc[:, at] = acc[:, at] + value

    view_tiles = {}

    def view_heads(heads):
        linked = jnp.concatenate(
            [
                jnp.zeros((1, ROWS), F32),
                jnp.broadcast_to(jnp.where(vl[:, 0:1] == 1, 0.0, FAR).astype(F32), (1, ROWS)),
                jnp.broadcast_to(jnp.where(vl[:, 1:2] == 1, 0.0, FAR).astype(F32), (1, ROWS)),
            ],
            axis=1,
        )
        attend_heads(heads, q_own, kv_all.at[0], kv_all.at[1], linked, emit_view, view_tiles)

    xy0 = permute_in(0)
    xy1 = permute_in(1)
    r0 = time_heads(0, xy0)
    xy2 = permute_in(2)
    r1 = time_heads(1, xy1)
    f0 = permute_back(0, r0)
    for copy in view_copies:
        copy.wait_recv()
    view_heads(range(8))
    r2 = time_heads(2, xy2)
    f1 = permute_back(1, r1)
    view_heads(range(8, HEADS))
    f2 = permute_back(2, r2)
    finish(0, f0)
    finish(1, f1)
    finish(2, f2)
    for copy in sent + box_copies + pair_copies + view_copies:
        copy.wait_send()


def on_device(qkv, cross_q, box_kv, null_kv, view_link, box_counts, box_visible):
    parts = len(PARTS)
    dma = pltpu.SemaphoreType.DMA
    wide = (ROWS, WIDTH)
    blended = pl.pallas_call(
        kernel,
        out_shape=jax.ShapeDtypeStruct(wide, BF16),
        in_specs=[pl.BlockSpec(memory_space=pl.ANY)] * 7,
        out_specs=pl.BlockSpec(memory_space=pltpu.VMEM),
        scratch_shapes=[
            pltpu.VMEM(wide, BF16),
            pltpu.VMEM((2, 3 * ROWS, WIDTH), BF16),
            pltpu.VMEM((3,) + wide, BF16),
            pltpu.VMEM((3,) + wide, BF16),
            pltpu.VMEM((3,) + wide, BF16),
            pltpu.VMEM(wide, BF16),
            pltpu.VMEM(wide, BF16),
            pltpu.VMEM(wide, BF16),
            pltpu.VMEM(wide, BF16),
            pltpu.VMEM(wide, BF16),
            pltpu.VMEM((8, 2, 8, WIDTH), BF16),
            pltpu.VMEM((2, WIDTH), BF16),
            pltpu.VMEM((2,) + wide, BF16),
            pltpu.VMEM((1, 2), jnp.int32),
            pltpu.VMEM((1, 1), jnp.int32),
            pltpu.VMEM((1, 64), jnp.int32),
            pltpu.VMEM((1, 128), jnp.int32),
            pltpu.VMEM(wide, F32),
            dma((9,)),
            dma((parts, 7)),
            dma((parts, 7)),
            dma((parts, 3)),
            dma((parts, 3)),
            dma((parts, 3)),
            dma((parts, 3)),
            dma((parts, 7)),
            dma((parts, 7)),
            dma((2,)),
            dma((2,)),
            dma((3,)),
            dma((3,)),
            dma((4,)),
            dma((4,)),
            dma((3, parts)),
        ],
        compiler_params=pltpu.CompilerParams(
            collective_id=0, has_side_effects=True, vmem_limit_bytes=40 << 20
        ),
        name="multiview_attention",
    )(
        qkv[:, 0, 0],
        cross_q[0, 0],
        box_kv[:, 0],
        null_kv,
        view_link,
        box_counts.reshape(1, 1),
        box_visible[0],
    )
    return blended[None, None]


def solution(mesh):
    return jax.shard_map(
        on_device,
        mesh=mesh,
        in_specs=(
            P(None, "cam", "frame", None, None),
            P("cam", "frame", None, None),
            P(None, "frame", "cam", None),
            P(None, None),
            P("cam", None),
            P("frame"),
            P("cam", "frame", None),
        ),
        out_specs=P("cam", "frame", None, None),
        check_vma=False,
    )
```

```python
import functools
import math

import jax
import jax.numpy as jnp
from jax import lax
from jax.experimental import pallas as pl
from jax.experimental.pallas import tpu as pltpu
from jax.sharding import PartitionSpec as P

MESH = pl.DeviceIdType.MESH
HEADS = 16
ROWS = 128
WIDTH = 1152
HEAD_DIM = WIDTH // HEADS
TILE = 128
SCALE = 1.0 / math.sqrt(HEAD_DIM)
FAR = -1e30
BF16 = jnp.bfloat16
F32 = jnp.float32
PARTS = ((0, 3), (3, 7), (7, 9))


def head_window(head):
    low = head * HEAD_DIM
    first = low // TILE
    last = (low + HEAD_DIM - 1) // TILE
    return low, first, last + 1


def heads_and_tiles():
    plan = []
    head_done = tile_done = 0
    for _, high in PARTS:
        heads = (high * TILE) // HEAD_DIM
        tiles = WIDTH // TILE if heads == HEADS else (heads * HEAD_DIM) // TILE
        plan.append((range(head_done, heads), (tile_done, tiles)))
        head_done, tile_done = heads, tiles
    return plan


def cols(first, last):
    return pl.ds(first * TILE, (last - first) * TILE)


def attend_heads(heads, q_ref, k_ref, v_ref, bias, emit, tiles):
    for head in heads:
        low, first, last = head_window(head)
        span = (last - first) * TILE
        lane = lax.broadcasted_iota(jnp.int32, (1, span), 1) + first * TILE
        mine = (lane >= low) & (lane < low + HEAD_DIM)
        window = pl.ds(first * TILE, span)
        q = q_ref[:, window] * mine.astype(F32).astype(BF16)
        scores = lax.dot_general(
            q, k_ref[:, window], (((1,), (1,)), ((), ())), preferred_element_type=F32
        )
        scores = scores + bias
        top = jnp.max(scores, axis=1, keepdims=True)
        weights = jnp.exp((scores - top) * SCALE)
        total = jnp.sum(weights, axis=1, keepdims=True)
        result = jnp.dot(weights.astype(BF16), v_ref[:, window], preferred_element_type=F32)
        result = result * (1.0 / total)
        for tile in range(first, last):
            at = (tile - first) * TILE
            part = result[:, at : at + TILE]
            if tile in tiles:
                part = jnp.where(mine[:, at : at + TILE], part, tiles[tile])
            tiles[tile] = part
            if low + HEAD_DIM >= (tile + 1) * TILE:
                emit(tile, tiles.pop(tile))


def kernel(
    qkv, cross_q, box_kv, null_kv, view_link, box_counts, box_visible, out,
    q_own, kv_all, z_in, near_out, near_in, far_out, early, home, t_out, t_in, t_group, t_fin,
    cq, boxes, nulls, ckv, vl, bc, bv, bv_wide, acc,
    local_sem, z_send, z_recv, xy_send, xy_recv, rxy_send, rxy_recv, rz_send, rz_recv,
    view_send, view_recv, box_send, box_recv, pair_send, pair_recv, own_sem,
):
    cam = lax.axis_index("cam")
    frame = lax.axis_index("frame")
    x, y, z = frame // 16, (frame // 8) % 2, frame % 8
    half = x % 2
    spot = half * 2 + y

    def z_peer(d):
        return (cam, x * 16 + y * 8 + (z + d) % 8)

    def spot_of(dx, dy):
        return ((half + dx) % 2) * 2 + (y + dy) % 2

    def xy_peer(dx, dy):
        return (cam, ((x // 2) * 2 + (half + dx) % 2) * 16 + ((y + dy) % 2) * 8 + z)

    def cam_peer(d):
        return ((cam + d) % 8, frame)

    pair = ((cam // 2) * 2 + (cam + 1) % 2, frame)
    z_order = (4, 3, 5, 2, 6, 1, 7)
    xy_order = ((1, 1), (0, 1), (1, 0))

    barrier = pltpu.get_barrier_semaphore()
    peers = [z_peer(d) for d in z_order] + [cam_peer(d) for d in (4, 2, 6, 1, 7)]
    peers += [xy_peer(*d) for d in xy_order]
    for peer in peers:
        pl.semaphore_signal(barrier, inc=1, device_id=peer, device_id_type=MESH)

    def rows16(i):
        return pl.ds(pl.multiple_of(i * 16, 16), 16)

    def rows32(i):
        return pl.ds(pl.multiple_of(i * 32, 32), 32)

    def local_copy(src, dst, sem):
        copy = pltpu.make_async_copy(src, dst, sem)
        copy.start()
        return copy

    local = []
    for src, dst in (
        (qkv.at[0], q_own),
        (qkv.at[pl.ds(1, 2)], kv_all.at[:, pl.ds(0, ROWS)]),
        (qkv.at[:, rows16(z)], z_in.at[:, rows16(z)]),
        (cross_q, cq),
        (box_kv, boxes.at[cam]),
        (null_kv, nulls),
        (view_link, vl),
        (box_counts, bc),
        (box_visible, bv),
    ):
        local.append(local_copy(src, dst, local_sem.at[len(local)]))

    row = lax.broadcasted_iota(jnp.int32, (ROWS, ROWS), 0)
    col = lax.broadcasted_iota(jnp.int32, (ROWS, ROWS), 1)

    def by_group(r):
        return ((r >> 2) & 7) * 16 + (r >> 5) * 4 + (r & 3)

    to_group = (col == by_group(row)).astype(F32).astype(BF16)
    to_frame = (row == by_group(col)).astype(F32).astype(BF16)
    same_patch = jnp.where(((row ^ col) & 3) == 0, 0.0, FAR).astype(F32)

    def reorder(matrix, values):
        return jnp.dot(matrix, values, preferred_element_type=F32)

    pl.semaphore_wait(barrier, len(peers))

    sent = []

    def remote(src, dst, send, recv, peer):
        copy = pltpu.make_async_remote_copy(
            src_ref=src, dst_ref=dst, send_sem=send, recv_sem=recv, device_id=peer,
            device_id_type=MESH,
        )
        copy.start()
        sent.append(copy)
        return copy

    def arrive(copies):
        for copy in copies:
            if any(copy is one for one in sent):
                copy.wait_recv()
            else:
                copy.wait()

    plan = heads_and_tiles()

    def send_z(part, source):
        at = cols(*PARTS[part])
        target = z_in if part == 0 else home
        copies = [
            remote(
                source.at[:, rows16((z + d) % 8), at], target.at[:, rows16(z), at],
                z_send.at[part, i], z_recv.at[part, i], z_peer(d),
            )
            for i, d in enumerate(z_order)
        ]
        if part > 0:
            copies.append(
                local_copy(
                    source.at[:, rows16(z), at], target.at[:, rows16(z), at], own_sem.at[0, part]
                )
            )
        return copies

    def send_xy(part):
        at = cols(*PARTS[part])
        target = early if part == 0 else near_in
        copies = [
            remote(
                near_out.at[:, rows32(spot_of(*d)), at], target.at[:, rows32(spot), at],
                xy_send.at[part, i], xy_recv.at[part, i], xy_peer(*d),
            )
            for i, d in enumerate(xy_order)
        ]
        copies.append(
            local_copy(
                near_out.at[:, rows32(spot), at], target.at[:, rows32(spot), at],
                own_sem.at[1, part],
            )
        )
        return copies

    def group_own(part):
        at = cols(*PARTS[part])
        near_out[0, :, at] = reorder(to_group, q_own[:, at]).astype(BF16)
        for t in range(2):
            near_out[t + 1, :, at] = reorder(to_group, kv_all[t, 0:ROWS, at]).astype(BF16)
        return send_xy(part)

    def group_first(copies):
        arrive(copies)
        at = cols(*PARTS[0])
        for t in range(3):
            near_out[t, :, at] = reorder(to_group, z_in[t, :, at]).astype(BF16)
        return send_xy(0)

    def spread(part, copies):
        arrive(copies)
        at = cols(*PARTS[part])
        for t in range(3):
            far_out[t, :, at] = reorder(to_frame, near_in[t, :, at]).astype(BF16)
        return send_z(part, far_out)

    half_tiles = {}

    def emit_time(tile, value):
        t_out[:, cols(tile, tile + 1)] = value.astype(BF16)

    def time_heads(part, copies):
        arrive(copies)
        if part == 0:
            at = cols(*PARTS[0])
            for t in range(3):
                home[t, :, at] = reorder(to_frame, early[t, :, at]).astype(BF16)
        heads, tiles = plan[part]
        attend_heads(heads, home.at[0], home.at[1], home.at[2], same_patch, emit_time, half_tiles)
        at = cols(*tiles)
        back = [
            remote(
                t_out.at[rows16((z + d) % 8), at], t_in.at[rows16(z), at],
                rz_send.at[part, i], rz_recv.at[part, i], z_peer(d),
            )
            for i, d in enumerate(z_order)
        ]
        back.append(
            local_copy(t_out.at[rows16(z), at], t_in.at[rows16(z), at], own_sem.at[2, part])
        )
        return back

    def group_back(part, copies):
        arrive(copies)
        at = cols(*plan[part][1])
        t_group[:, at] = reorder(to_group, t_in[:, at]).astype(BF16)
        back = [
            remote(
                t_group.at[rows32(spot_of(*d)), at], t_fin.at[rows32(spot), at],
                rxy_send.at[part, i], rxy_recv.at[part, i], xy_peer(*d),
            )
            for i, d in enumerate(xy_order)
        ]
        back.append(
            local_copy(t_group.at[rows32(spot), at], t_fin.at[rows32(spot), at], own_sem.at[3, part])
        )
        return back

    def finish(part, copies):
        arrive(copies)
        at = cols(*plan[part][1])
        out[:, at] = (acc[:, at] + reorder(to_frame, t_fin[:, at])).astype(BF16)

    def cross_attention(copies):
        arrive(copies)
        ckv[...] = jnp.zeros_like(ckv)
        for t in range(2):
            slots = jnp.concatenate([boxes[c, t].astype(F32) for c in range(8)], axis=0)
            ckv[t, 0:64, :] = slots.astype(BF16)
            first_row = lax.broadcasted_iota(jnp.int32, (16, WIDTH), 0) == 0
            null_row = jnp.broadcast_to(nulls[t : t + 1, :].astype(F32), (16, WIDTH))
            ckv[t, 64:80, :] = jnp.where(first_row, null_row, 0.0).astype(BF16)
        bv_wide[...] = jnp.zeros_like(bv_wide)
        bv_wide[:, 0:64] = bv[...]
        lane = lax.broadcasted_iota(jnp.int32, (1, ROWS), 1)
        live = ((lane < bc[...]) & (bv_wide[...] == 1)) | (lane == 64)
        cross_bias = jnp.where(live, 0.0, FAR).astype(F32)

        def emit_cross(tile, value):
            acc[:, cols(tile, tile + 1)] = value

        attend_heads(range(HEADS), cq, ckv.at[0], ckv.at[1], cross_bias, emit_cross, {})

    def emit_view(tile, value):
        at = cols(tile, tile + 1)
        acc[:, at] = acc[:, at] + value

    view_tiles = {}

    def view_heads(heads):
        linked = jnp.concatenate(
            [
                jnp.zeros((1, ROWS), F32),
                jnp.broadcast_to(jnp.where(vl[:, 0:1] == 1, 0.0, FAR).astype(F32), (1, ROWS)),
                jnp.broadcast_to(jnp.where(vl[:, 1:2] == 1, 0.0, FAR).astype(F32), (1, ROWS)),
            ],
            axis=1,
        )
        attend_heads(heads, q_own, kv_all.at[0], kv_all.at[1], linked, emit_view, view_tiles)

    z0 = send_z(0, qkv)
    arrive(local[0:2])
    xy1 = group_own(1)
    xy2 = group_own(2)
    box_copies = [
        remote(box_kv, boxes.at[cam], box_send.at[i], box_recv.at[i], cam_peer(d))
        for i, d in enumerate((2, 6, 4))
    ]
    pair_copies = [remote(box_kv, boxes.at[cam], pair_send.at[0], pair_recv.at[0], pair)]
    view_copies = [
        remote(
            qkv.at[pl.ds(1, 2)], kv_all.at[:, pl.ds(ROWS * (i + 1), ROWS)],
            view_send.at[i], view_recv.at[i], cam_peer(d),
        )
        for i, d in enumerate((1, 7))
    ]
    z1 = spread(1, xy1)
    arrive(box_copies)
    for i, d in enumerate((2, 6, 4)):
        block = boxes.at[(cam + 8 - d) % 8]
        pair_copies.append(
            remote(block, block, pair_send.at[i + 1], pair_recv.at[i + 1], pair)
        )
    z2 = spread(2, xy2)
    cross_attention(local[3:] + pair_copies)
    xy0 = group_first(z0 + local[2:3])
    r0 = time_heads(0, xy0)
    arrive(view_copies)
    view_heads(range(5))
    r1 = time_heads(1, z1)
    f0 = group_back(0, r0)
    view_heads(range(5, 10))
    r2 = time_heads(2, z2)
    f1 = group_back(1, r1)
    view_heads(range(10, HEADS))
    f2 = group_back(2, r2)
    finish(0, f0)
    finish(1, f1)
    finish(2, f2)
    for copy in sent:
        copy.wait_send()


def on_device(qkv, cross_q, box_kv, null_kv, view_link, box_counts, box_visible):
    parts = len(PARTS)
    dma = pltpu.SemaphoreType.DMA
    wide = (ROWS, WIDTH)
    blended = pl.pallas_call(
        kernel,
        out_shape=jax.ShapeDtypeStruct(wide, BF16),
        in_specs=[pl.BlockSpec(memory_space=pltpu.HBM)] * 7,
        out_specs=pl.BlockSpec(memory_space=pltpu.VMEM),
        scratch_shapes=[
            pltpu.VMEM(wide, BF16),
            pltpu.VMEM((2, 3 * ROWS, WIDTH), BF16),
            pltpu.VMEM((3,) + wide, BF16),
            pltpu.VMEM((3,) + wide, BF16),
            pltpu.VMEM((3,) + wide, BF16),
            pltpu.VMEM((3,) + wide, BF16),
            pltpu.VMEM((3,) + wide, BF16),
            pltpu.VMEM((3,) + wide, BF16),
            pltpu.VMEM(wide, BF16),
            pltpu.VMEM(wide, BF16),
            pltpu.VMEM(wide, BF16),
            pltpu.VMEM(wide, BF16),
            pltpu.VMEM(wide, BF16),
            pltpu.VMEM((8, 2, 8, WIDTH), BF16),
            pltpu.VMEM((2, WIDTH), BF16),
            pltpu.VMEM((2,) + wide, BF16),
            pltpu.VMEM((1, 2), jnp.int32),
            pltpu.VMEM((1, 1), jnp.int32),
            pltpu.VMEM((1, 64), jnp.int32),
            pltpu.VMEM((1, 128), jnp.int32),
            pltpu.VMEM(wide, F32),
            dma((9,)),
            dma((parts, 7)),
            dma((parts, 7)),
            dma((parts, 3)),
            dma((parts, 3)),
            dma((parts, 3)),
            dma((parts, 3)),
            dma((parts, 7)),
            dma((parts, 7)),
            dma((2,)),
            dma((2,)),
            dma((3,)),
            dma((3,)),
            dma((4,)),
            dma((4,)),
            dma((4, parts)),
        ],
        compiler_params=pltpu.CompilerParams(
            collective_id=0, has_side_effects=True, vmem_limit_bytes=56 << 20
        ),
        name="multiview_attention",
    )(
        qkv[:, 0, 0],
        cross_q[0, 0],
        box_kv[:, 0],
        null_kv,
        view_link,
        box_counts.reshape(1, 1),
        box_visible[0],
    )
    return blended[None, None]


def solution(mesh):
    return jax.shard_map(
        on_device,
        mesh=mesh,
        in_specs=(
            P(None, "cam", "frame", None, None),
            P("cam", "frame", None, None),
            P(None, "frame", "cam", None),
            P(None, None),
            P("cam", None),
            P("frame"),
            P("cam", "frame", None),
        ),
        out_specs=P("cam", "frame", None, None),
        check_vma=False,
    )
```

```python
import functools
import math

import jax
import jax.numpy as jnp
from jax import lax
from jax.experimental import pallas as pl
from jax.experimental.pallas import tpu as pltpu
from jax.sharding import PartitionSpec as P

MESH = pl.DeviceIdType.MESH
HEADS = 16
ROWS = 128
WIDTH = 1152
HEAD_DIM = WIDTH // HEADS
TILE = 128
SCALE = 1.0 / math.sqrt(HEAD_DIM)
FAR = -1e30
BF16 = jnp.bfloat16
F32 = jnp.float32
PARTS = ((0, 3), (3, 7), (7, 9))
VIEW_PIECES = ((0, 3), (3, 6), (6, 9))


def head_window(head):
    low = head * HEAD_DIM
    first = low // TILE
    last = (low + HEAD_DIM - 1) // TILE
    return low, first, last + 1


def heads_and_tiles():
    plan = []
    head_done = tile_done = 0
    for _, high in PARTS:
        heads = (high * TILE) // HEAD_DIM
        tiles = WIDTH // TILE if heads == HEADS else (heads * HEAD_DIM) // TILE
        plan.append((range(head_done, heads), (tile_done, tiles)))
        head_done, tile_done = heads, tiles
    return plan


def cols(first, last):
    return pl.ds(first * TILE, (last - first) * TILE)


GROUP = 8


def attend_heads(heads, q_ref, k_ref, v_ref, bias, emit, tiles):
    heads = list(heads)
    for start in range(0, len(heads), GROUP):
        group = heads[start : start + GROUP]
        windows, owned, scores = [], [], []
        for head in group:
            low, first, last = head_window(head)
            span = (last - first) * TILE
            lane = lax.broadcasted_iota(jnp.int32, (1, span), 1) + first * TILE
            mine = (lane >= low) & (lane < low + HEAD_DIM)
            window = pl.ds(first * TILE, span)
            q = q_ref[:, window] * mine.astype(F32).astype(BF16)
            windows.append(window)
            owned.append(mine)
            scores.append(
                lax.dot_general(
                    q, k_ref[:, window], (((1,), (1,)), ((), ())), preferred_element_type=F32
                )
            )
        scores = [score + bias for score in scores]
        tops = [jnp.max(score, axis=1, keepdims=True) for score in scores]
        weights = [jnp.exp((score - top) * SCALE) for score, top in zip(scores, tops)]
        totals = [jnp.sum(weight, axis=1, keepdims=True) for weight in weights]
        results = [
            jnp.dot(weight.astype(BF16), v_ref[:, window], preferred_element_type=F32)
            for weight, window in zip(weights, windows)
        ]
        results = [result * (1.0 / total) for result, total in zip(results, totals)]
        for head, mine, result in zip(group, owned, results):
            low, first, last = head_window(head)
            for tile in range(first, last):
                at = (tile - first) * TILE
                part = result[:, at : at + TILE]
                if tile in tiles:
                    part = jnp.where(mine[:, at : at + TILE], part, tiles[tile])
                tiles[tile] = part
                if low + HEAD_DIM >= (tile + 1) * TILE:
                    emit(tile, tiles.pop(tile))


def kernel(
    qkv, cross_q, box_kv, null_kv, view_link, box_counts, box_visible, out,
    q_own, kv_all, z_in, near_out, near_in, far_out, early, home, t_out, t_in, t_group, t_fin,
    cq, boxes, nulls, ckv, vl, bc, bv, bv_wide, acc,
    local_sem, z_send, z_recv, xy_send, xy_recv, rxy_send, rxy_recv, rz_send, rz_recv,
    view_send, view_recv, box_send, box_recv, pair_send, pair_recv, own_sem,
):
    cam = lax.axis_index("cam")
    frame = lax.axis_index("frame")
    x, y, z = frame // 16, (frame // 8) % 2, frame % 8
    half = x % 2
    spot = half * 2 + y

    def z_peer(d):
        return (cam, x * 16 + y * 8 + (z + d) % 8)

    def spot_of(dx, dy):
        return ((half + dx) % 2) * 2 + (y + dy) % 2

    def xy_peer(dx, dy):
        return (cam, ((x // 2) * 2 + (half + dx) % 2) * 16 + ((y + dy) % 2) * 8 + z)

    def cam_peer(d):
        return ((cam + d) % 8, frame)

    pair = ((cam // 2) * 2 + (cam + 1) % 2, frame)
    z_order = (4, 3, 5, 2, 6, 1, 7)
    xy_order = ((1, 1), (0, 1), (1, 0))

    barrier = pltpu.get_barrier_semaphore()
    peers = [z_peer(d) for d in z_order] + [cam_peer(d) for d in (4, 2, 6, 1, 7)]
    peers += [xy_peer(*d) for d in xy_order]
    for peer in peers:
        pl.semaphore_signal(barrier, inc=1, device_id=peer, device_id_type=MESH)

    def rows16(i):
        return pl.ds(pl.multiple_of(i * 16, 16), 16)

    def rows32(i):
        return pl.ds(pl.multiple_of(i * 32, 32), 32)

    def local_copy(src, dst, sem):
        copy = pltpu.make_async_copy(src, dst, sem)
        copy.start()
        return copy

    local = []
    for src, dst in (
        (qkv.at[0], q_own),
        (qkv.at[pl.ds(1, 2)], kv_all.at[:, pl.ds(0, ROWS)]),
        (qkv.at[:, rows16(z)], z_in.at[:, rows16(z)]),
        (cross_q, cq),
        (box_kv, boxes.at[cam]),
        (null_kv, nulls),
        (view_link, vl),
        (box_counts, bc),
        (box_visible, bv),
    ):
        local.append(local_copy(src, dst, local_sem.at[len(local)]))

    row = lax.broadcasted_iota(jnp.int32, (ROWS, ROWS), 0)
    col = lax.broadcasted_iota(jnp.int32, (ROWS, ROWS), 1)

    def by_group(r):
        return ((r >> 2) & 7) * 16 + (r >> 5) * 4 + (r & 3)

    to_group = (col == by_group(row)).astype(F32).astype(BF16)
    to_frame = (row == by_group(col)).astype(F32).astype(BF16)
    same_patch = jnp.where(((row ^ col) & 3) == 0, 0.0, FAR).astype(F32)

    def reorder(matrix, values):
        return jnp.dot(matrix, values, preferred_element_type=F32)

    pl.semaphore_wait(barrier, len(peers))

    sent = []

    def remote(src, dst, send, recv, peer):
        copy = pltpu.make_async_remote_copy(
            src_ref=src, dst_ref=dst, send_sem=send, recv_sem=recv, device_id=peer,
            device_id_type=MESH,
        )
        copy.start()
        sent.append(copy)
        return copy

    def arrive(copies):
        for copy in copies:
            if any(copy is one for one in sent):
                copy.wait_recv()
            else:
                copy.wait()

    plan = heads_and_tiles()

    def send_z(part, source):
        at = cols(*PARTS[part])
        target = z_in if part == 0 else home
        copies = [
            remote(
                source.at[:, rows16((z + d) % 8), at], target.at[:, rows16(z), at],
                z_send.at[part, i], z_recv.at[part, i], z_peer(d),
            )
            for i, d in enumerate(z_order)
        ]
        if part > 0:
            copies.append(
                local_copy(
                    source.at[:, rows16(z), at], target.at[:, rows16(z), at], own_sem.at[0, part]
                )
            )
        return copies

    def send_xy(part):
        at = cols(*PARTS[part])
        target = early if part == 0 else near_in
        copies = [
            remote(
                near_out.at[:, rows32(spot_of(*d)), at], target.at[:, rows32(spot), at],
                xy_send.at[part, i], xy_recv.at[part, i], xy_peer(*d),
            )
            for i, d in enumerate(xy_order)
        ]
        copies.append(
            local_copy(
                near_out.at[:, rows32(spot), at], target.at[:, rows32(spot), at],
                own_sem.at[1, part],
            )
        )
        return copies

    def group_own(part):
        at = cols(*PARTS[part])
        near_out[0, :, at] = reorder(to_group, q_own[:, at]).astype(BF16)
        for t in range(2):
            near_out[t + 1, :, at] = reorder(to_group, kv_all[t, 0:ROWS, at]).astype(BF16)
        return send_xy(part)

    def group_first(copies):
        arrive(copies)
        at = cols(*PARTS[0])
        for t in range(3):
            near_out[t, :, at] = reorder(to_group, z_in[t, :, at]).astype(BF16)
        return send_xy(0)

    def spread(part, copies):
        arrive(copies)
        at = cols(*PARTS[part])
        for t in range(3):
            far_out[t, :, at] = reorder(to_frame, near_in[t, :, at]).astype(BF16)
        return send_z(part, far_out)

    half_tiles = {}

    def emit_time(tile, value):
        t_out[:, cols(tile, tile + 1)] = value.astype(BF16)

    def time_heads(part, copies):
        arrive(copies)
        if part == 0:
            at = cols(*PARTS[0])
            for t in range(3):
                home[t, :, at] = reorder(to_frame, early[t, :, at]).astype(BF16)
        heads, tiles = plan[part]
        attend_heads(heads, home.at[0], home.at[1], home.at[2], same_patch, emit_time, half_tiles)
        at = cols(*tiles)
        back = [
            remote(
                t_out.at[rows16((z + d) % 8), at], t_in.at[rows16(z), at],
                rz_send.at[part, i], rz_recv.at[part, i], z_peer(d),
            )
            for i, d in enumerate(z_order)
        ]
        back.append(
            local_copy(t_out.at[rows16(z), at], t_in.at[rows16(z), at], own_sem.at[2, part])
        )
        return back

    def group_back(part, copies):
        arrive(copies)
        at = cols(*plan[part][1])
        t_group[:, at] = reorder(to_group, t_in[:, at]).astype(BF16)
        back = [
            remote(
                t_group.at[rows32(spot_of(*d)), at], t_fin.at[rows32(spot), at],
                rxy_send.at[part, i], rxy_recv.at[part, i], xy_peer(*d),
            )
            for i, d in enumerate(xy_order)
        ]
        back.append(
            local_copy(t_group.at[rows32(spot), at], t_fin.at[rows32(spot), at], own_sem.at[3, part])
        )
        return back

    def finish(part, copies):
        arrive(copies)
        at = cols(*plan[part][1])
        out[:, at] = (acc[:, at] + reorder(to_frame, t_fin[:, at])).astype(BF16)

    def cross_attention(copies):
        arrive(copies)
        ckv[...] = jnp.zeros_like(ckv)
        for t in range(2):
            slots = jnp.concatenate([boxes[c, t].astype(F32) for c in range(8)], axis=0)
            ckv[t, 0:64, :] = slots.astype(BF16)
            first_row = lax.broadcasted_iota(jnp.int32, (16, WIDTH), 0) == 0
            null_row = jnp.broadcast_to(nulls[t : t + 1, :].astype(F32), (16, WIDTH))
            ckv[t, 64:80, :] = jnp.where(first_row, null_row, 0.0).astype(BF16)
        bv_wide[...] = jnp.zeros_like(bv_wide)
        bv_wide[:, 0:64] = bv[...]
        lane = lax.broadcasted_iota(jnp.int32, (1, ROWS), 1)
        live = ((lane < bc[...]) & (bv_wide[...] == 1)) | (lane == 64)
        cross_bias = jnp.where(live, 0.0, FAR).astype(F32)

        def emit_cross(tile, value):
            acc[:, cols(tile, tile + 1)] = value

        attend_heads(range(HEADS), cq, ckv.at[0], ckv.at[1], cross_bias, emit_cross, {})

    def emit_view(tile, value):
        at = cols(tile, tile + 1)
        acc[:, at] = acc[:, at] + value

    view_tiles = {}

    def view_heads(heads):
        linked = jnp.concatenate(
            [
                jnp.zeros((1, ROWS), F32),
                jnp.broadcast_to(jnp.where(vl[:, 0:1] == 1, 0.0, FAR).astype(F32), (1, ROWS)),
                jnp.broadcast_to(jnp.where(vl[:, 1:2] == 1, 0.0, FAR).astype(F32), (1, ROWS)),
            ],
            axis=1,
        )
        attend_heads(heads, q_own, kv_all.at[0], kv_all.at[1], linked, emit_view, view_tiles)

    odd = cam % 2
    far_peer = ((cam + 7 - 6 * odd) % 8, frame)

    def view_rows(slot):
        return pl.ds(pl.multiple_of(slot * ROWS, ROWS), ROWS)

    def send_far_view(piece):
        at = cols(*VIEW_PIECES[piece])
        return remote(
            qkv.at[pl.ds(1, 2), :, at], kv_all.at[:, view_rows(2 - odd), at],
            view_send.at[piece + 1], view_recv.at[piece + 1], far_peer,
        )

    z0 = send_z(0, qkv)
    arrive(local[0:2])
    xy1 = group_own(1)
    xy2 = group_own(2)
    box_copies = [
        remote(box_kv, boxes.at[cam], box_send.at[i], box_recv.at[i], cam_peer(d))
        for i, d in enumerate((2, 6, 4))
    ]
    pair_copies = [remote(box_kv, boxes.at[cam], pair_send.at[0], pair_recv.at[0], pair)]
    view_copies = [
        remote(
            qkv.at[pl.ds(1, 2)], kv_all.at[:, view_rows(1 + odd)], view_send.at[0],
            view_recv.at[0], pair,
        )
    ]
    z1 = spread(1, xy1)
    z2 = spread(2, xy2)
    arrive(box_copies)
    for i, d in enumerate((2, 6, 4)):
        block = boxes.at[(cam + 8 - d) % 8]
        pair_copies.append(
            remote(block, block, pair_send.at[i + 1], pair_recv.at[i + 1], pair)
        )
    xy0 = group_first(z0 + local[2:3])
    for piece in range(len(VIEW_PIECES)):
        view_copies.append(send_far_view(piece))
    cross_attention(local[3:] + pair_copies)
    r0 = time_heads(0, xy0)
    r1 = time_heads(1, z1)
    arrive(view_copies[0:2])
    view_heads(range(0, 5))
    r2 = time_heads(2, z2)
    arrive(view_copies[2:3])
    view_heads(range(5, 10))
    f0 = group_back(0, r0)
    f1 = group_back(1, r1)
    arrive(view_copies[3:4])
    view_heads(range(10, HEADS))
    f2 = group_back(2, r2)
    finish(0, f0)
    finish(1, f1)
    finish(2, f2)
    for copy in sent:
        copy.wait_send()


def on_device(qkv, cross_q, box_kv, null_kv, view_link, box_counts, box_visible):
    parts = len(PARTS)
    dma = pltpu.SemaphoreType.DMA
    wide = (ROWS, WIDTH)
    blended = pl.pallas_call(
        kernel,
        out_shape=jax.ShapeDtypeStruct(wide, BF16),
        in_specs=[pl.BlockSpec(memory_space=pltpu.HBM)] * 7,
        out_specs=pl.BlockSpec(memory_space=pltpu.VMEM),
        scratch_shapes=[
            pltpu.VMEM(wide, BF16),
            pltpu.VMEM((2, 3 * ROWS, WIDTH), BF16),
            pltpu.VMEM((3,) + wide, BF16),
            pltpu.VMEM((3,) + wide, BF16),
            pltpu.VMEM((3,) + wide, BF16),
            pltpu.VMEM((3,) + wide, BF16),
            pltpu.VMEM((3,) + wide, BF16),
            pltpu.VMEM((3,) + wide, BF16),
            pltpu.VMEM(wide, BF16),
            pltpu.VMEM(wide, BF16),
            pltpu.VMEM(wide, BF16),
            pltpu.VMEM(wide, BF16),
            pltpu.VMEM(wide, BF16),
            pltpu.VMEM((8, 2, 8, WIDTH), BF16),
            pltpu.VMEM((2, WIDTH), BF16),
            pltpu.VMEM((2,) + wide, BF16),
            pltpu.VMEM((1, 2), jnp.int32),
            pltpu.VMEM((1, 1), jnp.int32),
            pltpu.VMEM((1, 64), jnp.int32),
            pltpu.VMEM((1, 128), jnp.int32),
            pltpu.VMEM(wide, F32),
            dma((9,)),
            dma((parts, 7)),
            dma((parts, 7)),
            dma((parts, 3)),
            dma((parts, 3)),
            dma((parts, 3)),
            dma((parts, 3)),
            dma((parts, 7)),
            dma((parts, 7)),
            dma((1 + len(VIEW_PIECES),)),
            dma((1 + len(VIEW_PIECES),)),
            dma((3,)),
            dma((3,)),
            dma((4,)),
            dma((4,)),
            dma((4, parts)),
        ],
        compiler_params=pltpu.CompilerParams(
            collective_id=0, has_side_effects=True, vmem_limit_bytes=56 << 20
        ),
        name="multiview_attention",
    )(
        qkv[:, 0, 0],
        cross_q[0, 0],
        box_kv[:, 0],
        null_kv,
        view_link,
        box_counts.reshape(1, 1),
        box_visible[0],
    )
    return blended[None, None]


def solution(mesh):
    return jax.shard_map(
        on_device,
        mesh=mesh,
        in_specs=(
            P(None, "cam", "frame", None, None),
            P("cam", "frame", None, None),
            P(None, "frame", "cam", None),
            P(None, None),
            P("cam", None),
            P("frame"),
            P("cam", "frame", None),
        ),
        out_specs=P("cam", "frame", None, None),
        check_vma=False,
    )
```

```python
import functools
import math

import jax
import jax.numpy as jnp
from jax import lax
from jax.experimental import pallas as pl
from jax.experimental.pallas import tpu as pltpu
from jax.sharding import PartitionSpec as P

MESH = pl.DeviceIdType.MESH
HEADS = 16
ROWS = 128
WIDTH = 1152
HEAD_DIM = WIDTH // HEADS
TILE = 128
SCALE = 1.0 / math.sqrt(HEAD_DIM)
FAR = -1e30
BF16 = jnp.bfloat16
F32 = jnp.float32
PARTS = ((0, 3), (3, 7), (7, 9))
VIEW_PIECES = ((0, 3), (3, 6), (6, 9))


def head_window(head):
    low = head * HEAD_DIM
    first = low // TILE
    last = (low + HEAD_DIM - 1) // TILE
    return low, first, last + 1


def heads_and_tiles():
    plan = []
    head_done = tile_done = 0
    for _, high in PARTS:
        heads = (high * TILE) // HEAD_DIM
        tiles = WIDTH // TILE if heads == HEADS else (heads * HEAD_DIM) // TILE
        plan.append((range(head_done, heads), (tile_done, tiles)))
        head_done, tile_done = heads, tiles
    return plan


def cols(first, last):
    return pl.ds(first * TILE, (last - first) * TILE)


GROUP = 8


def attend_heads(heads, q_ref, k_ref, v_ref, bias, emit, tiles):
    heads = list(heads)
    for start in range(0, len(heads), GROUP):
        group = heads[start : start + GROUP]
        windows, owned, scores = [], [], []
        for head in group:
            low, first, last = head_window(head)
            span = (last - first) * TILE
            lane = lax.broadcasted_iota(jnp.int32, (1, span), 1) + first * TILE
            mine = (lane >= low) & (lane < low + HEAD_DIM)
            window = pl.ds(first * TILE, span)
            q = q_ref[:, window] * mine.astype(F32).astype(BF16)
            windows.append(window)
            owned.append(mine)
            scores.append(
                lax.dot_general(
                    q, k_ref[:, window], (((1,), (1,)), ((), ())), preferred_element_type=F32
                )
            )
        scores = [score + bias for score in scores]
        tops = [jnp.max(score, axis=1, keepdims=True) for score in scores]
        weights = [jnp.exp((score - top) * SCALE) for score, top in zip(scores, tops)]
        totals = [jnp.sum(weight, axis=1, keepdims=True) for weight in weights]
        results = [
            jnp.dot(weight.astype(BF16), v_ref[:, window], preferred_element_type=F32)
            for weight, window in zip(weights, windows)
        ]
        results = [result * (1.0 / total) for result, total in zip(results, totals)]
        for head, mine, result in zip(group, owned, results):
            low, first, last = head_window(head)
            for tile in range(first, last):
                at = (tile - first) * TILE
                part = result[:, at : at + TILE]
                if tile in tiles:
                    part = jnp.where(mine[:, at : at + TILE], part, tiles[tile])
                tiles[tile] = part
                if low + HEAD_DIM >= (tile + 1) * TILE:
                    emit(tile, tiles.pop(tile))


def kernel(
    qkv, cross_q, box_kv, null_kv, view_link, box_counts, box_visible, out,
    q_own, kv_all, z_in, near_out, near_in, far_out, early, home, t_out, t_in, t_group, t_fin,
    cq, boxes, nulls, ckv, vl, bc, bv, bv_wide, acc,
    local_sem, z_send, z_recv, xy_send, xy_recv, rxy_send, rxy_recv, rz_send, rz_recv,
    view_send, view_recv, box_send, box_recv, pair_send, pair_recv, own_sem,
):
    cam = lax.axis_index("cam")
    frame = lax.axis_index("frame")
    x, y, z = frame // 16, (frame // 8) % 2, frame % 8
    half = x % 2
    spot = half * 2 + y

    def z_peer(d):
        return (cam, x * 16 + y * 8 + (z + d) % 8)

    def spot_of(dx, dy):
        return ((half + dx) % 2) * 2 + (y + dy) % 2

    def xy_peer(dx, dy):
        return (cam, ((x // 2) * 2 + (half + dx) % 2) * 16 + ((y + dy) % 2) * 8 + z)

    def cam_peer(d):
        return ((cam + d) % 8, frame)

    pair = ((cam // 2) * 2 + (cam + 1) % 2, frame)
    z_order = (4, 3, 5, 2, 6, 1, 7)
    xy_order = ((1, 1), (0, 1), (1, 0))

    barrier = pltpu.get_barrier_semaphore()
    peers = [z_peer(d) for d in z_order] + [cam_peer(d) for d in (4, 2, 6, 1, 7)]
    peers += [xy_peer(*d) for d in xy_order]
    for peer in peers:
        pl.semaphore_signal(barrier, inc=1, device_id=peer, device_id_type=MESH)

    def rows16(i):
        return pl.ds(pl.multiple_of(i * 16, 16), 16)

    def rows32(i):
        return pl.ds(pl.multiple_of(i * 32, 32), 32)

    def local_copy(src, dst, sem):
        copy = pltpu.make_async_copy(src, dst, sem)
        copy.start()
        return copy

    local = [
        local_copy(qkv.at[0], q_own, local_sem.at[0]),
        local_copy(qkv.at[pl.ds(1, 2)], kv_all.at[:, pl.ds(0, ROWS)], local_sem.at[1]),
    ]

    row = lax.broadcasted_iota(jnp.int32, (ROWS, ROWS), 0)
    col = lax.broadcasted_iota(jnp.int32, (ROWS, ROWS), 1)

    def by_group(r):
        return ((r >> 2) & 7) * 16 + (r >> 5) * 4 + (r & 3)

    to_group = (col == by_group(row)).astype(F32).astype(BF16)
    to_frame = (row == by_group(col)).astype(F32).astype(BF16)
    same_patch = jnp.where(((row ^ col) & 3) == 0, 0.0, FAR).astype(F32)

    def reorder(matrix, values):
        return jnp.dot(matrix, values, preferred_element_type=F32)

    pl.semaphore_wait(barrier, len(peers))

    sent = []
    drained = []

    def drain(copies):
        for copy in copies:
            if any(copy is one for one in sent) and not any(copy is one for one in drained):
                copy.wait_send()
                drained.append(copy)

    def remote(src, dst, send, recv, peer):
        copy = pltpu.make_async_remote_copy(
            src_ref=src, dst_ref=dst, send_sem=send, recv_sem=recv, device_id=peer,
            device_id_type=MESH,
        )
        copy.start()
        sent.append(copy)
        return copy

    def arrive(copies):
        for copy in copies:
            if any(copy is one for one in sent):
                copy.wait_recv()
            else:
                copy.wait()

    plan = heads_and_tiles()

    def send_z(part, source):
        at = cols(*PARTS[part])
        target = z_in if part == 0 else home
        copies = [
            remote(
                source.at[:, rows16((z + d) % 8), at], target.at[:, rows16(z), at],
                z_send.at[part, i], z_recv.at[part, i], z_peer(d),
            )
            for i, d in enumerate(z_order)
        ]
        if part > 0:
            copies.append(
                local_copy(
                    source.at[:, rows16(z), at], target.at[:, rows16(z), at], own_sem.at[0, part]
                )
            )
        return copies

    def send_xy(part):
        at = cols(*PARTS[part])
        target = early if part == 0 else near_in
        copies = [
            remote(
                near_out.at[:, rows32(spot_of(*d)), at], target.at[:, rows32(spot), at],
                xy_send.at[part, i], xy_recv.at[part, i], xy_peer(*d),
            )
            for i, d in enumerate(xy_order)
        ]
        copies.append(
            local_copy(
                near_out.at[:, rows32(spot), at], target.at[:, rows32(spot), at],
                own_sem.at[1, part],
            )
        )
        return copies

    def group_own(part):
        at = cols(*PARTS[part])
        near_out[0, :, at] = reorder(to_group, q_own[:, at]).astype(BF16)
        for t in range(2):
            near_out[t + 1, :, at] = reorder(to_group, kv_all[t, 0:ROWS, at]).astype(BF16)
        return send_xy(part)

    def group_first(copies):
        arrive(copies)
        at = cols(*PARTS[0])
        for t in range(3):
            near_out[t, :, at] = reorder(to_group, z_in[t, :, at]).astype(BF16)
        return send_xy(0)

    def spread(part, copies):
        arrive(copies)
        at = cols(*PARTS[part])
        for t in range(3):
            far_out[t, :, at] = reorder(to_frame, near_in[t, :, at]).astype(BF16)
        return send_z(part, far_out)

    half_tiles = {}

    def emit_time(tile, value):
        t_out[:, cols(tile, tile + 1)] = value.astype(BF16)

    def time_heads(part, copies):
        arrive(copies)
        if part == 0:
            at = cols(*PARTS[0])
            for t in range(3):
                home[t, :, at] = reorder(to_frame, early[t, :, at]).astype(BF16)
        heads, tiles = plan[part]
        attend_heads(heads, home.at[0], home.at[1], home.at[2], same_patch, emit_time, half_tiles)
        at = cols(*tiles)
        back = [
            remote(
                t_out.at[rows16((z + d) % 8), at], t_in.at[rows16(z), at],
                rz_send.at[part, i], rz_recv.at[part, i], z_peer(d),
            )
            for i, d in enumerate(z_order)
        ]
        back.append(
            local_copy(t_out.at[rows16(z), at], t_in.at[rows16(z), at], own_sem.at[2, part])
        )
        return back

    def group_back(part, copies):
        arrive(copies)
        at = cols(*plan[part][1])
        t_group[:, at] = reorder(to_group, t_in[:, at]).astype(BF16)
        back = [
            remote(
                t_group.at[rows32(spot_of(*d)), at], t_fin.at[rows32(spot), at],
                rxy_send.at[part, i], rxy_recv.at[part, i], xy_peer(*d),
            )
            for i, d in enumerate(xy_order)
        ]
        back.append(
            local_copy(t_group.at[rows32(spot), at], t_fin.at[rows32(spot), at], own_sem.at[3, part])
        )
        return back

    def finish(part, copies):
        arrive(copies)
        at = cols(*plan[part][1])
        out[:, at] = (acc[:, at] + reorder(to_frame, t_fin[:, at])).astype(BF16)

    def cross_attention(copies):
        arrive(copies)
        ckv[...] = jnp.zeros_like(ckv)
        for t in range(2):
            slots = jnp.concatenate([boxes[c, t].astype(F32) for c in range(8)], axis=0)
            ckv[t, 0:64, :] = slots.astype(BF16)
            first_row = lax.broadcasted_iota(jnp.int32, (16, WIDTH), 0) == 0
            null_row = jnp.broadcast_to(nulls[t : t + 1, :].astype(F32), (16, WIDTH))
            ckv[t, 64:80, :] = jnp.where(first_row, null_row, 0.0).astype(BF16)
        bv_wide[...] = jnp.zeros_like(bv_wide)
        bv_wide[:, 0:64] = bv[...]
        lane = lax.broadcasted_iota(jnp.int32, (1, ROWS), 1)
        live = ((lane < bc[...]) & (bv_wide[...] == 1)) | (lane == 64)
        cross_bias = jnp.where(live, 0.0, FAR).astype(F32)

        def emit_cross(tile, value):
            acc[:, cols(tile, tile + 1)] = value

        attend_heads(range(HEADS), cq, ckv.at[0], ckv.at[1], cross_bias, emit_cross, {})

    def emit_view(tile, value):
        at = cols(tile, tile + 1)
        acc[:, at] = acc[:, at] + value

    view_tiles = {}

    def view_heads(heads):
        linked = jnp.concatenate(
            [
                jnp.zeros((1, ROWS), F32),
                jnp.broadcast_to(jnp.where(vl[:, 0:1] == 1, 0.0, FAR).astype(F32), (1, ROWS)),
                jnp.broadcast_to(jnp.where(vl[:, 1:2] == 1, 0.0, FAR).astype(F32), (1, ROWS)),
            ],
            axis=1,
        )
        attend_heads(heads, q_own, kv_all.at[0], kv_all.at[1], linked, emit_view, view_tiles)

    odd = cam % 2
    far_peer = ((cam + 7 - 6 * odd) % 8, frame)

    def view_rows(slot):
        return pl.ds(pl.multiple_of(slot * ROWS, ROWS), ROWS)

    def send_far_view(piece):
        at = cols(*VIEW_PIECES[piece])
        return remote(
            qkv.at[pl.ds(1, 2), :, at], kv_all.at[:, view_rows(2 - odd), at],
            view_send.at[piece + 1], view_recv.at[piece + 1], far_peer,
        )

    z0 = send_z(0, qkv)
    for src, dst in (
        (qkv.at[:, rows16(z)], z_in.at[:, rows16(z)]),
        (cross_q, cq),
        (box_kv, boxes.at[cam]),
        (null_kv, nulls),
        (view_link, vl),
        (box_counts, bc),
        (box_visible, bv),
    ):
        local.append(local_copy(src, dst, local_sem.at[len(local)]))
    box_copies = [
        remote(box_kv, boxes.at[cam], box_send.at[i], box_recv.at[i], cam_peer(d))
        for i, d in enumerate((2, 6, 4))
    ]
    pair_copies = [remote(box_kv, boxes.at[cam], pair_send.at[0], pair_recv.at[0], pair)]
    arrive(local[0:2])
    xy1 = group_own(1)
    xy2 = group_own(2)
    view_copies = [
        remote(
            qkv.at[pl.ds(1, 2)], kv_all.at[:, view_rows(1 + odd)], view_send.at[0],
            view_recv.at[0], pair,
        )
    ]
    z1 = spread(1, xy1)
    z2 = spread(2, xy2)
    arrive(box_copies)
    for i, d in enumerate((2, 6, 4)):
        block = boxes.at[(cam + 8 - d) % 8]
        pair_copies.append(
            remote(block, block, pair_send.at[i + 1], pair_recv.at[i + 1], pair)
        )
    xy0 = group_first(z0 + local[2:3])
    for piece in range(len(VIEW_PIECES)):
        view_copies.append(send_far_view(piece))
    cross_attention(local[3:] + pair_copies)
    r0 = time_heads(0, xy0)
    r1 = time_heads(1, z1)
    arrive(view_copies[0:2])
    view_heads(range(0, 5))
    drain(z0 + xy1 + xy2 + box_copies + pair_copies)
    r2 = time_heads(2, z2)
    arrive(view_copies[2:3])
    view_heads(range(5, 10))
    drain(z1 + xy0 + view_copies[0:2])
    f0 = group_back(0, r0)
    drain(z2 + r0 + view_copies)
    f1 = group_back(1, r1)
    arrive(view_copies[3:4])
    view_heads(range(10, HEADS))
    drain(r1 + f0)
    f2 = group_back(2, r2)
    finish(0, f0)
    finish(1, f1)
    drain(r2 + f1)
    finish(2, f2)
    drain(sent)


def in_hbm(operand):
    return pltpu.with_memory_space_constraint(operand, pltpu.HBM)


def on_device(qkv, cross_q, box_kv, null_kv, view_link, box_counts, box_visible):
    parts = len(PARTS)
    dma = pltpu.SemaphoreType.DMA
    wide = (ROWS, WIDTH)
    blended = pl.pallas_call(
        kernel,
        out_shape=jax.ShapeDtypeStruct(wide, BF16),
        in_specs=[pl.BlockSpec(memory_space=pl.ANY)] * 7,
        out_specs=pl.BlockSpec(memory_space=pltpu.VMEM),
        scratch_shapes=[
            pltpu.VMEM(wide, BF16),
            pltpu.VMEM((2, 3 * ROWS, WIDTH), BF16),
            pltpu.VMEM((3,) + wide, BF16),
            pltpu.VMEM((3,) + wide, BF16),
            pltpu.VMEM((3,) + wide, BF16),
            pltpu.VMEM((3,) + wide, BF16),
            pltpu.VMEM((3,) + wide, BF16),
            pltpu.VMEM((3,) + wide, BF16),
            pltpu.VMEM(wide, BF16),
            pltpu.VMEM(wide, BF16),
            pltpu.VMEM(wide, BF16),
            pltpu.VMEM(wide, BF16),
            pltpu.VMEM(wide, BF16),
            pltpu.VMEM((8, 2, 8, WIDTH), BF16),
            pltpu.VMEM((2, WIDTH), BF16),
            pltpu.VMEM((2,) + wide, BF16),
            pltpu.VMEM((1, 2), jnp.int32),
            pltpu.VMEM((1, 1), jnp.int32),
            pltpu.VMEM((1, 64), jnp.int32),
            pltpu.VMEM((1, 128), jnp.int32),
            pltpu.VMEM(wide, F32),
            dma((9,)),
            dma((parts, 7)),
            dma((parts, 7)),
            dma((parts, 3)),
            dma((parts, 3)),
            dma((parts, 3)),
            dma((parts, 3)),
            dma((parts, 7)),
            dma((parts, 7)),
            dma((1 + len(VIEW_PIECES),)),
            dma((1 + len(VIEW_PIECES),)),
            dma((3,)),
            dma((3,)),
            dma((4,)),
            dma((4,)),
            dma((4, parts)),
        ],
        compiler_params=pltpu.CompilerParams(
            collective_id=0, has_side_effects=True, vmem_limit_bytes=40 << 20
        ),
        name="multiview_attention",
    )(
        in_hbm(qkv[:, 0, 0]),
        in_hbm(cross_q[0, 0]),
        in_hbm(box_kv[:, 0]),
        in_hbm(null_kv),
        in_hbm(view_link),
        box_counts.reshape(1, 1),
        in_hbm(box_visible[0]),
    )
    return blended[None, None]


def solution(mesh):
    return jax.shard_map(
        on_device,
        mesh=mesh,
        in_specs=(
            P(None, "cam", "frame", None, None),
            P("cam", "frame", None, None),
            P(None, "frame", "cam", None),
            P(None, None),
            P("cam", None),
            P("frame"),
            P("cam", "frame", None),
        ),
        out_specs=P("cam", "frame", None, None),
        check_vma=False,
    )
```

```python
import functools
import math

import jax
import jax.numpy as jnp
from jax import lax
from jax.experimental import pallas as pl
from jax.experimental.pallas import tpu as pltpu
from jax.sharding import PartitionSpec as P

MESH = pl.DeviceIdType.MESH
HEADS = 16
ROWS = 128
WIDTH = 1152
HEAD_DIM = WIDTH // HEADS
TILE = 128
SCALE = 1.0 / math.sqrt(HEAD_DIM)
FAR = -1e30
BF16 = jnp.bfloat16
F32 = jnp.float32
PARTS = ((0, 3), (3, 7), (7, 9))
VIEW_PIECES = ((0, 3), (3, 7), (7, 9))


def head_window(head):
    low = head * HEAD_DIM
    first = low // TILE
    last = (low + HEAD_DIM - 1) // TILE
    return low, first, last + 1


def heads_and_tiles():
    plan = []
    head_done = tile_done = 0
    for _, high in PARTS:
        heads = (high * TILE) // HEAD_DIM
        tiles = WIDTH // TILE if heads == HEADS else (heads * HEAD_DIM) // TILE
        plan.append((range(head_done, heads), (tile_done, tiles)))
        head_done, tile_done = heads, tiles
    return plan


def cols(first, last):
    return pl.ds(first * TILE, (last - first) * TILE)


GROUP = 8


def attend_heads(heads, q_ref, k_ref, v_ref, bias, emit, tiles):
    heads = list(heads)
    for start in range(0, len(heads), GROUP):
        group = heads[start : start + GROUP]
        windows, owned, scores = [], [], []
        for head in group:
            low, first, last = head_window(head)
            span = (last - first) * TILE
            lane = lax.broadcasted_iota(jnp.int32, (1, span), 1) + first * TILE
            mine = (lane >= low) & (lane < low + HEAD_DIM)
            window = pl.ds(first * TILE, span)
            q = q_ref[:, window] * mine.astype(F32).astype(BF16)
            windows.append(window)
            owned.append(mine)
            scores.append(
                lax.dot_general(
                    q, k_ref[:, window], (((1,), (1,)), ((), ())), preferred_element_type=F32
                )
            )
        scores = [score + bias for score in scores]
        tops = [jnp.max(score, axis=1, keepdims=True) for score in scores]
        weights = [jnp.exp((score - top) * SCALE) for score, top in zip(scores, tops)]
        totals = [jnp.sum(weight, axis=1, keepdims=True) for weight in weights]
        results = [
            jnp.dot(weight.astype(BF16), v_ref[:, window], preferred_element_type=F32)
            for weight, window in zip(weights, windows)
        ]
        results = [result * (1.0 / total) for result, total in zip(results, totals)]
        for head, mine, result in zip(group, owned, results):
            low, first, last = head_window(head)
            for tile in range(first, last):
                at = (tile - first) * TILE
                part = result[:, at : at + TILE]
                if tile in tiles:
                    part = jnp.where(mine[:, at : at + TILE], part, tiles[tile])
                tiles[tile] = part
                if low + HEAD_DIM >= (tile + 1) * TILE:
                    emit(tile, tiles.pop(tile))


def kernel(
    qkv, cross_q, box_kv, null_kv, view_link, box_counts, box_visible, out,
    q_own, kv_all, z_in, near_out, near_in, far_out, early, home, t_out, t_in, t_group, t_fin,
    cq, boxes, nulls, ckv, vl, bc, bv, bv_wide, acc,
    local_sem, z_send, z_recv, xy_send, xy_recv, rxy_send, rxy_recv, rz_send, rz_recv,
    view_send, view_recv, box_send, box_recv, pair_send, pair_recv, own_sem,
):
    cam = lax.axis_index("cam")
    frame = lax.axis_index("frame")
    x, y, z = frame // 16, (frame // 8) % 2, frame % 8
    half = x % 2
    spot = half * 2 + y

    def z_peer(d):
        return (cam, x * 16 + y * 8 + (z + d) % 8)

    def spot_of(dx, dy):
        return ((half + dx) % 2) * 2 + (y + dy) % 2

    def xy_peer(dx, dy):
        return (cam, ((x // 2) * 2 + (half + dx) % 2) * 16 + ((y + dy) % 2) * 8 + z)

    def cam_peer(d):
        return ((cam + d) % 8, frame)

    pair = ((cam // 2) * 2 + (cam + 1) % 2, frame)
    z_order = (4, 3, 5, 2, 6, 1, 7)
    xy_order = ((1, 1), (0, 1), (1, 0))

    barrier = pltpu.get_barrier_semaphore()
    peers = [z_peer(d) for d in z_order] + [cam_peer(d) for d in (4, 2, 6, 1, 7)]
    peers += [xy_peer(*d) for d in xy_order]
    for peer in peers:
        pl.semaphore_signal(barrier, inc=1, device_id=peer, device_id_type=MESH)

    def rows16(i):
        return pl.ds(pl.multiple_of(i * 16, 16), 16)

    def rows32(i):
        return pl.ds(pl.multiple_of(i * 32, 32), 32)

    def local_copy(src, dst, sem):
        copy = pltpu.make_async_copy(src, dst, sem)
        copy.start()
        return copy

    local = [
        local_copy(qkv.at[0], q_own, local_sem.at[0]),
        local_copy(qkv.at[pl.ds(1, 2)], kv_all.at[:, pl.ds(0, ROWS)], local_sem.at[1]),
    ]

    row = lax.broadcasted_iota(jnp.int32, (ROWS, ROWS), 0)
    col = lax.broadcasted_iota(jnp.int32, (ROWS, ROWS), 1)

    def by_group(r):
        return ((r >> 2) & 7) * 16 + (r >> 5) * 4 + (r & 3)

    to_group = (col == by_group(row)).astype(F32).astype(BF16)
    to_frame = (row == by_group(col)).astype(F32).astype(BF16)
    same_patch = jnp.where(((row ^ col) & 3) == 0, 0.0, FAR).astype(F32)

    def reorder(matrix, values):
        return jnp.dot(matrix, values, preferred_element_type=F32)

    pl.semaphore_wait(barrier, len(peers))

    sent = []
    drained = []

    def drain(copies):
        for copy in copies:
            if any(copy is one for one in sent) and not any(copy is one for one in drained):
                copy.wait_send()
                drained.append(copy)

    def remote(src, dst, send, recv, peer):
        copy = pltpu.make_async_remote_copy(
            src_ref=src, dst_ref=dst, send_sem=send, recv_sem=recv, device_id=peer,
            device_id_type=MESH,
        )
        copy.start()
        sent.append(copy)
        return copy

    def arrive(copies):
        for copy in copies:
            if any(copy is one for one in sent):
                copy.wait_recv()
            else:
                copy.wait()

    plan = heads_and_tiles()

    def send_z(part, source):
        at = cols(*PARTS[part])
        target = z_in if part == 0 else home
        copies = [
            remote(
                source.at[:, rows16((z + d) % 8), at], target.at[:, rows16(z), at],
                z_send.at[part, i], z_recv.at[part, i], z_peer(d),
            )
            for i, d in enumerate(z_order)
        ]
        if part > 0:
            copies.append(
                local_copy(
                    source.at[:, rows16(z), at], target.at[:, rows16(z), at], own_sem.at[0, part]
                )
            )
        return copies

    def send_xy(part):
        at = cols(*PARTS[part])
        target = early if part == 0 else near_in
        copies = [
            remote(
                near_out.at[:, rows32(spot_of(*d)), at], target.at[:, rows32(spot), at],
                xy_send.at[part, i], xy_recv.at[part, i], xy_peer(*d),
            )
            for i, d in enumerate(xy_order)
        ]
        copies.append(
            local_copy(
                near_out.at[:, rows32(spot), at], target.at[:, rows32(spot), at],
                own_sem.at[1, part],
            )
        )
        return copies

    def group_own(part):
        at = cols(*PARTS[part])
        near_out[0, :, at] = reorder(to_group, q_own[:, at]).astype(BF16)
        for t in range(2):
            near_out[t + 1, :, at] = reorder(to_group, kv_all[t, 0:ROWS, at]).astype(BF16)
        return send_xy(part)

    def group_first(copies):
        arrive(copies)
        at = cols(*PARTS[0])
        for t in range(3):
            near_out[t, :, at] = reorder(to_group, z_in[t, :, at]).astype(BF16)
        return send_xy(0)

    def spread(part, copies):
        arrive(copies)
        at = cols(*PARTS[part])
        for t in range(3):
            far_out[t, :, at] = reorder(to_frame, near_in[t, :, at]).astype(BF16)
        return send_z(part, far_out)

    half_tiles = {}

    def emit_time(tile, value):
        t_out[:, cols(tile, tile + 1)] = value.astype(BF16)

    def time_heads(part, copies):
        arrive(copies)
        if part == 0:
            at = cols(*PARTS[0])
            for t in range(3):
                home[t, :, at] = reorder(to_frame, early[t, :, at]).astype(BF16)
        heads, tiles = plan[part]
        attend_heads(heads, home.at[0], home.at[1], home.at[2], same_patch, emit_time, half_tiles)
        at = cols(*tiles)
        back = [
            remote(
                t_out.at[rows16((z + d) % 8), at], t_in.at[rows16(z), at],
                rz_send.at[part, i], rz_recv.at[part, i], z_peer(d),
            )
            for i, d in enumerate(z_order)
        ]
        back.append(
            local_copy(t_out.at[rows16(z), at], t_in.at[rows16(z), at], own_sem.at[2, part])
        )
        return back

    def group_back(part, copies):
        arrive(copies)
        at = cols(*plan[part][1])
        t_group[:, at] = reorder(to_group, t_in[:, at]).astype(BF16)
        back = [
            remote(
                t_group.at[rows32(spot_of(*d)), at], t_fin.at[rows32(spot), at],
                rxy_send.at[part, i], rxy_recv.at[part, i], xy_peer(*d),
            )
            for i, d in enumerate(xy_order)
        ]
        back.append(
            local_copy(t_group.at[rows32(spot), at], t_fin.at[rows32(spot), at], own_sem.at[3, part])
        )
        return back

    def finish(part, copies):
        arrive(copies)
        at = cols(*plan[part][1])
        out[:, at] = (acc[:, at] + reorder(to_frame, t_fin[:, at])).astype(BF16)

    def cross_attention(copies):
        arrive(copies)
        ckv[...] = jnp.zeros_like(ckv)
        for t in range(2):
            slots = jnp.concatenate([boxes[c, t].astype(F32) for c in range(8)], axis=0)
            ckv[t, 0:64, :] = slots.astype(BF16)
            first_row = lax.broadcasted_iota(jnp.int32, (16, WIDTH), 0) == 0
            null_row = jnp.broadcast_to(nulls[t : t + 1, :].astype(F32), (16, WIDTH))
            ckv[t, 64:80, :] = jnp.where(first_row, null_row, 0.0).astype(BF16)
        bv_wide[...] = jnp.zeros_like(bv_wide)
        bv_wide[:, 0:64] = bv[...]
        lane = lax.broadcasted_iota(jnp.int32, (1, ROWS), 1)
        live = ((lane < bc[...]) & (bv_wide[...] == 1)) | (lane == 64)
        cross_bias = jnp.where(live, 0.0, FAR).astype(F32)

        def emit_cross(tile, value):
            acc[:, cols(tile, tile + 1)] = value

        attend_heads(range(HEADS), cq, ckv.at[0], ckv.at[1], cross_bias, emit_cross, {})

    def emit_view(tile, value):
        at = cols(tile, tile + 1)
        acc[:, at] = acc[:, at] + value

    view_tiles = {}

    def view_heads(heads):
        linked = jnp.concatenate(
            [
                jnp.zeros((1, ROWS), F32),
                jnp.broadcast_to(jnp.where(vl[:, 0:1] == 1, 0.0, FAR).astype(F32), (1, ROWS)),
                jnp.broadcast_to(jnp.where(vl[:, 1:2] == 1, 0.0, FAR).astype(F32), (1, ROWS)),
            ],
            axis=1,
        )
        attend_heads(heads, q_own, kv_all.at[0], kv_all.at[1], linked, emit_view, view_tiles)

    odd = cam % 2
    far_peer = ((cam + 7 - 6 * odd) % 8, frame)

    def view_rows(slot):
        return pl.ds(pl.multiple_of(slot * ROWS, ROWS), ROWS)

    def send_far_view(piece):
        at = cols(*VIEW_PIECES[piece])
        return remote(
            qkv.at[pl.ds(1, 2), :, at], kv_all.at[:, view_rows(2 - odd), at],
            view_send.at[piece + 1], view_recv.at[piece + 1], far_peer,
        )

    z0 = send_z(0, qkv)
    for src, dst in (
        (qkv.at[:, rows16(z)], z_in.at[:, rows16(z)]),
        (cross_q, cq),
        (box_kv, boxes.at[cam]),
        (null_kv, nulls),
        (view_link, vl),
        (box_counts, bc),
        (box_visible, bv),
    ):
        local.append(local_copy(src, dst, local_sem.at[len(local)]))
    arrive(local[0:2])
    xy1 = group_own(1)
    xy2 = group_own(2)
    box_copies = [
        remote(box_kv, boxes.at[cam], box_send.at[i], box_recv.at[i], cam_peer(d))
        for i, d in enumerate((2, 6, 4))
    ]
    pair_copies = [remote(box_kv, boxes.at[cam], pair_send.at[0], pair_recv.at[0], pair)]
    view_copies = [
        remote(
            qkv.at[pl.ds(1, 2)], kv_all.at[:, view_rows(1 + odd)], view_send.at[0],
            view_recv.at[0], pair,
        )
    ]
    z1 = spread(1, xy1)
    z2 = spread(2, xy2)
    xy0 = group_first(z0 + local[2:3])
    for piece in range(len(VIEW_PIECES)):
        view_copies.append(send_far_view(piece))
    arrive(box_copies)
    for i, d in enumerate((2, 6, 4)):
        block = boxes.at[(cam + 8 - d) % 8]
        pair_copies.append(
            remote(block, block, pair_send.at[i + 1], pair_recv.at[i + 1], pair)
        )
    r0 = time_heads(0, xy0)
    r1 = time_heads(1, z1)
    cross_attention(local[3:] + pair_copies)
    r2 = time_heads(2, z2)
    drain(z0 + xy1 + xy2 + box_copies + pair_copies)
    arrive(view_copies[0:2])
    view_heads(range(0, 5))
    f0 = group_back(0, r0)
    drain(z1 + xy0 + view_copies[0:2])
    arrive(view_copies[2:3])
    view_heads(range(5, 12))
    f1 = group_back(1, r1)
    drain(z2 + r0 + view_copies)
    arrive(view_copies[3:4])
    view_heads(range(12, HEADS))
    drain(r1 + f0)
    f2 = group_back(2, r2)
    finish(0, f0)
    finish(1, f1)
    drain(r2 + f1)
    finish(2, f2)
    drain(sent)


def in_hbm(operand):
    return pltpu.with_memory_space_constraint(operand, pltpu.HBM)


def on_device(qkv, cross_q, box_kv, null_kv, view_link, box_counts, box_visible):
    parts = len(PARTS)
    dma = pltpu.SemaphoreType.DMA
    wide = (ROWS, WIDTH)
    blended = pl.pallas_call(
        kernel,
        out_shape=jax.ShapeDtypeStruct(wide, BF16),
        in_specs=[pl.BlockSpec(memory_space=pl.ANY)] * 7,
        out_specs=pl.BlockSpec(memory_space=pltpu.VMEM),
        scratch_shapes=[
            pltpu.VMEM(wide, BF16),
            pltpu.VMEM((2, 3 * ROWS, WIDTH), BF16),
            pltpu.VMEM((3,) + wide, BF16),
            pltpu.VMEM((3,) + wide, BF16),
            pltpu.VMEM((3,) + wide, BF16),
            pltpu.VMEM((3,) + wide, BF16),
            pltpu.VMEM((3,) + wide, BF16),
            pltpu.VMEM((3,) + wide, BF16),
            pltpu.VMEM(wide, BF16),
            pltpu.VMEM(wide, BF16),
            pltpu.VMEM(wide, BF16),
            pltpu.VMEM(wide, BF16),
            pltpu.VMEM(wide, BF16),
            pltpu.VMEM((8, 2, 8, WIDTH), BF16),
            pltpu.VMEM((2, WIDTH), BF16),
            pltpu.VMEM((2,) + wide, BF16),
            pltpu.VMEM((1, 2), jnp.int32),
            pltpu.VMEM((1, 1), jnp.int32),
            pltpu.VMEM((1, 64), jnp.int32),
            pltpu.VMEM((1, 128), jnp.int32),
            pltpu.VMEM(wide, F32),
            dma((9,)),
            dma((parts, 7)),
            dma((parts, 7)),
            dma((parts, 3)),
            dma((parts, 3)),
            dma((parts, 3)),
            dma((parts, 3)),
            dma((parts, 7)),
            dma((parts, 7)),
            dma((1 + len(VIEW_PIECES),)),
            dma((1 + len(VIEW_PIECES),)),
            dma((3,)),
            dma((3,)),
            dma((4,)),
            dma((4,)),
            dma((4, parts)),
        ],
        compiler_params=pltpu.CompilerParams(
            collective_id=0, has_side_effects=True, vmem_limit_bytes=40 << 20
        ),
        name="multiview_attention",
    )(
        in_hbm(qkv[:, 0, 0]),
        in_hbm(cross_q[0, 0]),
        in_hbm(box_kv[:, 0]),
        in_hbm(null_kv),
        in_hbm(view_link),
        box_counts.reshape(1, 1),
        in_hbm(box_visible[0]),
    )
    return blended[None, None]


def solution(mesh):
    return jax.shard_map(
        on_device,
        mesh=mesh,
        in_specs=(
            P(None, "cam", "frame", None, None),
            P("cam", "frame", None, None),
            P(None, "frame", "cam", None),
            P(None, None),
            P("cam", None),
            P("frame"),
            P("cam", "frame", None),
        ),
        out_specs=P("cam", "frame", None, None),
        check_vma=False,
    )
```

```python
import functools
import math

import jax
import jax.numpy as jnp
from jax import lax
from jax.experimental import pallas as pl
from jax.experimental.pallas import tpu as pltpu
from jax.sharding import PartitionSpec as P

MESH = pl.DeviceIdType.MESH
HEADS = 16
ROWS = 128
WIDTH = 1152
HEAD_DIM = WIDTH // HEADS
TILE = 128
SCALE = 1.0 / math.sqrt(HEAD_DIM)
FAR = -1e30
BF16 = jnp.bfloat16
F32 = jnp.float32
PARTS = ((0, 3), (3, 7), (7, 9))
VIEW_PIECES = ((0, 3), (3, 7), (7, 9))


def head_window(head):
    low = head * HEAD_DIM
    first = low // TILE
    last = (low + HEAD_DIM - 1) // TILE
    return low, first, last + 1


def heads_and_tiles():
    plan = []
    head_done = tile_done = 0
    for _, high in PARTS:
        heads = (high * TILE) // HEAD_DIM
        tiles = WIDTH // TILE if heads == HEADS else (heads * HEAD_DIM) // TILE
        plan.append((range(head_done, heads), (tile_done, tiles)))
        head_done, tile_done = heads, tiles
    return plan


def cols(first, last):
    return pl.ds(first * TILE, (last - first) * TILE)


GROUP = 8


def attend_heads(heads, q_ref, k_ref, v_ref, bias, emit, tiles):
    heads = list(heads)
    for start in range(0, len(heads), GROUP):
        group = heads[start : start + GROUP]
        windows, owned, scores = [], [], []
        for head in group:
            low, first, last = head_window(head)
            span = (last - first) * TILE
            lane = lax.broadcasted_iota(jnp.int32, (1, span), 1) + first * TILE
            mine = (lane >= low) & (lane < low + HEAD_DIM)
            window = pl.ds(first * TILE, span)
            q = q_ref[:, window] * mine.astype(F32).astype(BF16)
            windows.append(window)
            owned.append(mine)
            scores.append(
                lax.dot_general(
                    q, k_ref[:, window], (((1,), (1,)), ((), ())), preferred_element_type=F32
                )
            )
        scores = [score + bias for score in scores]
        tops = [jnp.max(score, axis=1, keepdims=True) for score in scores]
        weights = [jnp.exp((score - top) * SCALE) for score, top in zip(scores, tops)]
        totals = [jnp.sum(weight, axis=1, keepdims=True) for weight in weights]
        results = [
            jnp.dot(weight.astype(BF16), v_ref[:, window], preferred_element_type=F32)
            for weight, window in zip(weights, windows)
        ]
        results = [result * (1.0 / total) for result, total in zip(results, totals)]
        for head, mine, result in zip(group, owned, results):
            low, first, last = head_window(head)
            for tile in range(first, last):
                at = (tile - first) * TILE
                part = result[:, at : at + TILE]
                if tile in tiles:
                    part = jnp.where(mine[:, at : at + TILE], part, tiles[tile])
                tiles[tile] = part
                if low + HEAD_DIM >= (tile + 1) * TILE:
                    emit(tile, tiles.pop(tile))


def kernel(
    qkv, cross_q, box_kv, null_kv, view_link, box_counts, box_visible, out,
    q_own, kv_all, z_in, near_out, near_in, far_out, early, home, t_out, t_in, t_group, t_fin,
    cq, boxes, nulls, ckv, vl, bc, bv, bv_wide, acc,
    local_sem, z_send, z_recv, xy_send, xy_recv, rxy_send, rxy_recv, rz_send, rz_recv,
    view_send, view_recv, box_send, box_recv, pair_send, pair_recv, own_sem,
):
    cam = lax.axis_index("cam")
    frame = lax.axis_index("frame")
    x, y, z = frame // 16, (frame // 8) % 2, frame % 8
    half = x % 2
    spot = half * 2 + y

    def z_peer(d):
        return (cam, x * 16 + y * 8 + (z + d) % 8)

    def spot_of(dx, dy):
        return ((half + dx) % 2) * 2 + (y + dy) % 2

    def xy_peer(dx, dy):
        return (cam, ((x // 2) * 2 + (half + dx) % 2) * 16 + ((y + dy) % 2) * 8 + z)

    def cam_peer(d):
        return ((cam + d) % 8, frame)

    pair = ((cam // 2) * 2 + (cam + 1) % 2, frame)
    z_order = (4, 3, 5, 2, 6, 1, 7)
    xy_order = ((1, 1), (0, 1), (1, 0))

    barrier = pltpu.get_barrier_semaphore()
    peers = [z_peer(d) for d in z_order] + [cam_peer(d) for d in (2, 6, 1, 7)]
    peers += [xy_peer(*d) for d in xy_order]
    for peer in peers:
        pl.semaphore_signal(barrier, inc=1, device_id=peer, device_id_type=MESH)

    def rows16(i):
        return pl.ds(pl.multiple_of(i * 16, 16), 16)

    def rows32(i):
        return pl.ds(pl.multiple_of(i * 32, 32), 32)

    def local_copy(src, dst, sem):
        copy = pltpu.make_async_copy(src, dst, sem)
        copy.start()
        return copy

    local = [
        local_copy(qkv.at[0], q_own, local_sem.at[0]),
        local_copy(qkv.at[pl.ds(1, 2)], kv_all.at[:, pl.ds(0, ROWS)], local_sem.at[1]),
    ]

    row = lax.broadcasted_iota(jnp.int32, (ROWS, ROWS), 0)
    col = lax.broadcasted_iota(jnp.int32, (ROWS, ROWS), 1)

    def by_group(r):
        return ((r >> 2) & 7) * 16 + (r >> 5) * 4 + (r & 3)

    to_group = (col == by_group(row)).astype(F32).astype(BF16)
    to_frame = (row == by_group(col)).astype(F32).astype(BF16)
    same_patch = jnp.where(((row ^ col) & 3) == 0, 0.0, FAR).astype(F32)

    def reorder(matrix, values):
        return jnp.dot(matrix, values, preferred_element_type=F32)

    pl.semaphore_wait(barrier, len(peers))

    sent = []
    drained = []

    def drain(copies):
        for copy in copies:
            if any(copy is one for one in sent) and not any(copy is one for one in drained):
                copy.wait_send()
                drained.append(copy)

    def remote(src, dst, send, recv, peer):
        copy = pltpu.make_async_remote_copy(
            src_ref=src, dst_ref=dst, send_sem=send, recv_sem=recv, device_id=peer,
            device_id_type=MESH,
        )
        copy.start()
        sent.append(copy)
        return copy

    def arrive(copies):
        for copy in copies:
            if any(copy is one for one in sent):
                copy.wait_recv()
            else:
                copy.wait()

    plan = heads_and_tiles()

    def send_z(part, source):
        at = cols(*PARTS[part])
        target = z_in if part == 0 else home
        copies = [
            remote(
                source.at[:, rows16((z + d) % 8), at], target.at[:, rows16(z), at],
                z_send.at[part, i], z_recv.at[part, i], z_peer(d),
            )
            for i, d in enumerate(z_order)
        ]
        if part > 0:
            copies.append(
                local_copy(
                    source.at[:, rows16(z), at], target.at[:, rows16(z), at], own_sem.at[0, part]
                )
            )
        return copies

    def send_xy(part):
        at = cols(*PARTS[part])
        target = early if part == 0 else near_in
        copies = [
            remote(
                near_out.at[:, rows32(spot_of(*d)), at], target.at[:, rows32(spot), at],
                xy_send.at[part, i], xy_recv.at[part, i], xy_peer(*d),
            )
            for i, d in enumerate(xy_order)
        ]
        copies.append(
            local_copy(
                near_out.at[:, rows32(spot), at], target.at[:, rows32(spot), at],
                own_sem.at[1, part],
            )
        )
        return copies

    def group_own(part):
        at = cols(*PARTS[part])
        near_out[0, :, at] = reorder(to_group, q_own[:, at]).astype(BF16)
        for t in range(2):
            near_out[t + 1, :, at] = reorder(to_group, kv_all[t, 0:ROWS, at]).astype(BF16)
        return send_xy(part)

    def group_first(copies):
        arrive(copies)
        at = cols(*PARTS[0])
        for t in range(3):
            near_out[t, :, at] = reorder(to_group, z_in[t, :, at]).astype(BF16)
        return send_xy(0)

    def spread(part, copies):
        arrive(copies)
        at = cols(*PARTS[part])
        for t in range(3):
            far_out[t, :, at] = reorder(to_frame, near_in[t, :, at]).astype(BF16)
        return send_z(part, far_out)

    half_tiles = {}

    def emit_time(tile, value):
        t_out[:, cols(tile, tile + 1)] = value.astype(BF16)

    def time_heads(part, copies):
        arrive(copies)
        if part == 0:
            at = cols(*PARTS[0])
            for t in range(3):
                home[t, :, at] = reorder(to_frame, early[t, :, at]).astype(BF16)
        heads, tiles = plan[part]
        attend_heads(heads, home.at[0], home.at[1], home.at[2], same_patch, emit_time, half_tiles)
        at = cols(*tiles)
        back = [
            remote(
                t_out.at[rows16((z + d) % 8), at], t_in.at[rows16(z), at],
                rz_send.at[part, i], rz_recv.at[part, i], z_peer(d),
            )
            for i, d in enumerate(z_order)
        ]
        back.append(
            local_copy(t_out.at[rows16(z), at], t_in.at[rows16(z), at], own_sem.at[2, part])
        )
        return back

    def group_back(part, copies):
        arrive(copies)
        at = cols(*plan[part][1])
        t_group[:, at] = reorder(to_group, t_in[:, at]).astype(BF16)
        back = [
            remote(
                t_group.at[rows32(spot_of(*d)), at], t_fin.at[rows32(spot), at],
                rxy_send.at[part, i], rxy_recv.at[part, i], xy_peer(*d),
            )
            for i, d in enumerate(xy_order)
        ]
        back.append(
            local_copy(t_group.at[rows32(spot), at], t_fin.at[rows32(spot), at], own_sem.at[3, part])
        )
        return back

    def finish(part, copies):
        arrive(copies)
        at = cols(*plan[part][1])
        out[:, at] = (acc[:, at] + reorder(to_frame, t_fin[:, at])).astype(BF16)

    def cross_attention(copies):
        arrive(copies)
        ckv[...] = jnp.zeros_like(ckv)
        for t in range(2):
            slots = jnp.concatenate([boxes[c, t].astype(F32) for c in range(8)], axis=0)
            ckv[t, 0:64, :] = slots.astype(BF16)
            first_row = lax.broadcasted_iota(jnp.int32, (16, WIDTH), 0) == 0
            null_row = jnp.broadcast_to(nulls[t : t + 1, :].astype(F32), (16, WIDTH))
            ckv[t, 64:80, :] = jnp.where(first_row, null_row, 0.0).astype(BF16)
        bv_wide[...] = jnp.zeros_like(bv_wide)
        bv_wide[:, 0:64] = bv[...]
        lane = lax.broadcasted_iota(jnp.int32, (1, ROWS), 1)
        live = ((lane < bc[...]) & (bv_wide[...] == 1)) | (lane == 64)
        cross_bias = jnp.where(live, 0.0, FAR).astype(F32)

        def emit_cross(tile, value):
            acc[:, cols(tile, tile + 1)] = value

        attend_heads(range(HEADS), cq, ckv.at[0], ckv.at[1], cross_bias, emit_cross, {})

    def emit_view(tile, value):
        at = cols(tile, tile + 1)
        acc[:, at] = acc[:, at] + value

    view_tiles = {}

    def view_heads(heads):
        linked = jnp.concatenate(
            [
                jnp.zeros((1, ROWS), F32),
                jnp.broadcast_to(jnp.where(vl[:, 0:1] == 1, 0.0, FAR).astype(F32), (1, ROWS)),
                jnp.broadcast_to(jnp.where(vl[:, 1:2] == 1, 0.0, FAR).astype(F32), (1, ROWS)),
            ],
            axis=1,
        )
        attend_heads(heads, q_own, kv_all.at[0], kv_all.at[1], linked, emit_view, view_tiles)

    odd = cam % 2
    far_peer = ((cam + 7 - 6 * odd) % 8, frame)

    def view_rows(slot):
        return pl.ds(pl.multiple_of(slot * ROWS, ROWS), ROWS)

    def send_far_view(piece):
        at = cols(*VIEW_PIECES[piece])
        return remote(
            qkv.at[pl.ds(1, 2), :, at], kv_all.at[:, view_rows(2 - odd), at],
            view_send.at[piece + 1], view_recv.at[piece + 1], far_peer,
        )

    z0 = send_z(0, qkv)
    for src, dst in (
        (qkv.at[:, rows16(z)], z_in.at[:, rows16(z)]),
        (cross_q, cq),
        (box_kv, boxes.at[cam]),
        (null_kv, nulls),
        (view_link, vl),
        (box_counts, bc),
        (box_visible, bv),
    ):
        local.append(local_copy(src, dst, local_sem.at[len(local)]))
    arrive(local[0:2])
    xy1 = group_own(1)
    xy2 = group_own(2)
    box_copies = [
        remote(box_kv, boxes.at[cam], box_send.at[i], box_recv.at[i], cam_peer(d))
        for i, d in enumerate((2, 6))
    ]
    pair_copies = [remote(box_kv, boxes.at[cam], pair_send.at[0], pair_recv.at[0], pair)]
    view_copies = [
        remote(
            qkv.at[pl.ds(1, 2)], kv_all.at[:, view_rows(1 + odd)], view_send.at[0],
            view_recv.at[0], pair,
        )
    ]
    z1 = spread(1, xy1)
    z2 = spread(2, xy2)
    xy0 = group_first(z0 + local[2:3])
    arrive(box_copies)
    for i, (d, t) in enumerate(((2, 0), (6, 1))):
        block = boxes.at[(cam + 8 - d) % 8, t]
        box_copies.append(
            remote(block, block, box_send.at[i + 2], box_recv.at[i + 2], cam_peer(d))
        )

    for piece in range(len(VIEW_PIECES)):
        view_copies.append(send_far_view(piece))
    def cross_chip(i, d):
        block = boxes.at[(cam + 8 - d) % 8]
        pair_copies.append(remote(block, block, pair_send.at[i], pair_recv.at[i], pair))

    cross_chip(1, 2)
    cross_chip(2, 6)
    r0 = time_heads(0, xy0)
    r1 = time_heads(1, z1)
    arrive(box_copies[2:4])
    cross_chip(3, 4)
    r2 = time_heads(2, z2)
    cross_attention(local[3:] + pair_copies)
    drain(z0 + xy1 + xy2 + box_copies + pair_copies)
    arrive(view_copies[0:2])
    view_heads(range(0, 5))
    f0 = group_back(0, r0)
    drain(z1 + xy0 + view_copies[0:2])
    arrive(view_copies[2:3])
    view_heads(range(5, 12))
    f1 = group_back(1, r1)
    drain(z2 + r0 + view_copies)
    arrive(view_copies[3:4])
    view_heads(range(12, HEADS))
    drain(r1 + f0)
    f2 = group_back(2, r2)
    finish(0, f0)
    finish(1, f1)
    drain(r2 + f1)
    finish(2, f2)
    drain(sent)


def in_hbm(operand):
    return pltpu.with_memory_space_constraint(operand, pltpu.HBM)


def on_device(qkv, cross_q, box_kv, null_kv, view_link, box_counts, box_visible):
    parts = len(PARTS)
    dma = pltpu.SemaphoreType.DMA
    wide = (ROWS, WIDTH)
    blended = pl.pallas_call(
        kernel,
        out_shape=jax.ShapeDtypeStruct(wide, BF16),
        in_specs=[pl.BlockSpec(memory_space=pl.ANY)] * 7,
        out_specs=pl.BlockSpec(memory_space=pltpu.VMEM),
        scratch_shapes=[
            pltpu.VMEM(wide, BF16),
            pltpu.VMEM((2, 3 * ROWS, WIDTH), BF16),
            pltpu.VMEM((3,) + wide, BF16),
            pltpu.VMEM((3,) + wide, BF16),
            pltpu.VMEM((3,) + wide, BF16),
            pltpu.VMEM((3,) + wide, BF16),
            pltpu.VMEM((3,) + wide, BF16),
            pltpu.VMEM((3,) + wide, BF16),
            pltpu.VMEM(wide, BF16),
            pltpu.VMEM(wide, BF16),
            pltpu.VMEM(wide, BF16),
            pltpu.VMEM(wide, BF16),
            pltpu.VMEM(wide, BF16),
            pltpu.VMEM((8, 2, 8, WIDTH), BF16),
            pltpu.VMEM((2, WIDTH), BF16),
            pltpu.VMEM((2,) + wide, BF16),
            pltpu.VMEM((1, 2), jnp.int32),
            pltpu.VMEM((1, 1), jnp.int32),
            pltpu.VMEM((1, 64), jnp.int32),
            pltpu.VMEM((1, 128), jnp.int32),
            pltpu.VMEM(wide, F32),
            dma((9,)),
            dma((parts, 7)),
            dma((parts, 7)),
            dma((parts, 3)),
            dma((parts, 3)),
            dma((parts, 3)),
            dma((parts, 3)),
            dma((parts, 7)),
            dma((parts, 7)),
            dma((1 + len(VIEW_PIECES),)),
            dma((1 + len(VIEW_PIECES),)),
            dma((4,)),
            dma((4,)),
            dma((4,)),
            dma((4,)),
            dma((4, parts)),
        ],
        compiler_params=pltpu.CompilerParams(
            collective_id=0, has_side_effects=True, vmem_limit_bytes=40 << 20
        ),
        name="multiview_attention",
    )(
        in_hbm(qkv[:, 0, 0]),
        in_hbm(cross_q[0, 0]),
        in_hbm(box_kv[:, 0]),
        in_hbm(null_kv),
        in_hbm(view_link),
        box_counts.reshape(1, 1),
        in_hbm(box_visible[0]),
    )
    return blended[None, None]


def solution(mesh):
    return jax.shard_map(
        on_device,
        mesh=mesh,
        in_specs=(
            P(None, "cam", "frame", None, None),
            P("cam", "frame", None, None),
            P(None, "frame", "cam", None),
            P(None, None),
            P("cam", None),
            P("frame"),
            P("cam", "frame", None),
        ),
        out_specs=P("cam", "frame", None, None),
        check_vma=False,
    )
```

```python
import functools
import math

import jax
import jax.numpy as jnp
from jax import lax
from jax.experimental import pallas as pl
from jax.experimental.pallas import tpu as pltpu
from jax.sharding import PartitionSpec as P

MESH = pl.DeviceIdType.MESH
HEADS = 16
ROWS = 128
WIDTH = 1152
HEAD_DIM = WIDTH // HEADS
TILE = 128
SCALE = 1.0 / math.sqrt(HEAD_DIM)
FAR = -1e30
BF16 = jnp.bfloat16
F32 = jnp.float32
PARTS = ((0, 3), (3, 7), (7, 9))
VIEW_PIECES = ((0, 3), (3, 7), (7, 9))


def head_window(head):
    low = head * HEAD_DIM
    first = low // TILE
    last = (low + HEAD_DIM - 1) // TILE
    return low, first, last + 1


def heads_and_tiles():
    plan = []
    head_done = tile_done = 0
    for _, high in PARTS:
        heads = (high * TILE) // HEAD_DIM
        tiles = WIDTH // TILE if heads == HEADS else (heads * HEAD_DIM) // TILE
        plan.append((range(head_done, heads), (tile_done, tiles)))
        head_done, tile_done = heads, tiles
    return plan


def cols(first, last):
    return pl.ds(first * TILE, (last - first) * TILE)


GROUP = 8


def attend_heads(heads, q_ref, k_ref, v_ref, bias, emit, tiles):
    heads = list(heads)
    for start in range(0, len(heads), GROUP):
        group = heads[start : start + GROUP]
        windows, owned, scores = [], [], []
        for head in group:
            low, first, last = head_window(head)
            span = (last - first) * TILE
            lane = lax.broadcasted_iota(jnp.int32, (1, span), 1) + first * TILE
            mine = (lane >= low) & (lane < low + HEAD_DIM)
            window = pl.ds(first * TILE, span)
            q = q_ref[:, window] * mine.astype(F32).astype(BF16)
            windows.append(window)
            owned.append(mine)
            scores.append(
                lax.dot_general(
                    q, k_ref[:, window], (((1,), (1,)), ((), ())), preferred_element_type=F32
                )
            )
        scores = [score + bias for score in scores]
        tops = [jnp.max(score, axis=1, keepdims=True) for score in scores]
        weights = [jnp.exp((score - top) * SCALE) for score, top in zip(scores, tops)]
        totals = [jnp.sum(weight, axis=1, keepdims=True) for weight in weights]
        results = [
            jnp.dot(weight.astype(BF16), v_ref[:, window], preferred_element_type=F32)
            for weight, window in zip(weights, windows)
        ]
        results = [result * (1.0 / total) for result, total in zip(results, totals)]
        for head, mine, result in zip(group, owned, results):
            low, first, last = head_window(head)
            for tile in range(first, last):
                at = (tile - first) * TILE
                part = result[:, at : at + TILE]
                if tile in tiles:
                    part = jnp.where(mine[:, at : at + TILE], part, tiles[tile])
                tiles[tile] = part
                if low + HEAD_DIM >= (tile + 1) * TILE:
                    emit(tile, tiles.pop(tile))


def kernel(
    qkv, cross_q, box_kv, null_kv, view_link, box_counts, box_visible, out,
    q_own, kv_all, z_in, near_out, near_in, far_out, early, home, t_out, t_in, t_group, t_fin,
    cq, boxes, nulls, ckv, vl, bc, bv, bv_wide, acc,
    local_sem, z_send, z_recv, xy_send, xy_recv, rxy_send, rxy_recv, rz_send, rz_recv,
    view_send, view_recv, box_send, box_recv, pair_send, pair_recv, own_sem,
):
    cam = lax.axis_index("cam")
    frame = lax.axis_index("frame")
    x, y, z = frame // 16, (frame // 8) % 2, frame % 8
    half = x % 2
    spot = half * 2 + y

    def z_peer(d):
        return (cam, x * 16 + y * 8 + (z + d) % 8)

    def spot_of(dx, dy):
        return ((half + dx) % 2) * 2 + (y + dy) % 2

    def xy_peer(dx, dy):
        return (cam, ((x // 2) * 2 + (half + dx) % 2) * 16 + ((y + dy) % 2) * 8 + z)

    def cam_peer(d):
        return ((cam + d) % 8, frame)

    pair = ((cam // 2) * 2 + (cam + 1) % 2, frame)
    z_order = (4, 3, 5, 2, 6, 1, 7)
    xy_order = ((1, 1), (0, 1), (1, 0))

    barrier = pltpu.get_barrier_semaphore()
    peers = [z_peer(d) for d in z_order] + [cam_peer(d) for d in (2, 6, 1, 7)]
    peers += [xy_peer(*d) for d in xy_order]
    for peer in peers:
        pl.semaphore_signal(barrier, inc=1, device_id=peer, device_id_type=MESH)

    def rows16(i):
        return pl.ds(pl.multiple_of(i * 16, 16), 16)

    def rows32(i):
        return pl.ds(pl.multiple_of(i * 32, 32), 32)

    def local_copy(src, dst, sem):
        copy = pltpu.make_async_copy(src, dst, sem)
        copy.start()
        return copy

    local = [
        local_copy(qkv.at[0], q_own, local_sem.at[0]),
        local_copy(qkv.at[pl.ds(1, 2)], kv_all.at[:, pl.ds(0, ROWS)], local_sem.at[1]),
    ]

    row = lax.broadcasted_iota(jnp.int32, (ROWS, ROWS), 0)
    col = lax.broadcasted_iota(jnp.int32, (ROWS, ROWS), 1)

    def by_group(r):
        return ((r >> 2) & 7) * 16 + (r >> 5) * 4 + (r & 3)

    to_group = (col == by_group(row)).astype(F32).astype(BF16)
    to_frame = (row == by_group(col)).astype(F32).astype(BF16)
    same_patch = jnp.where(((row ^ col) & 3) == 0, 0.0, FAR).astype(F32)

    def reorder(matrix, values):
        return jnp.dot(matrix, values, preferred_element_type=F32)

    pl.semaphore_wait(barrier, len(peers))

    sent = []
    drained = []

    def drain(copies):
        for copy in copies:
            if any(copy is one for one in sent) and not any(copy is one for one in drained):
                copy.wait_send()
                drained.append(copy)

    def remote(src, dst, send, recv, peer):
        copy = pltpu.make_async_remote_copy(
            src_ref=src, dst_ref=dst, send_sem=send, recv_sem=recv, device_id=peer,
            device_id_type=MESH,
        )
        copy.start()
        sent.append(copy)
        return copy

    def arrive(copies):
        for copy in copies:
            if any(copy is one for one in sent):
                copy.wait_recv()
            else:
                copy.wait()

    plan = heads_and_tiles()

    def send_z(part, source):
        at = cols(*PARTS[part])
        target = z_in if part == 0 else home
        copies = [
            remote(
                source.at[:, rows16((z + d) % 8), at], target.at[:, rows16(z), at],
                z_send.at[part, i], z_recv.at[part, i], z_peer(d),
            )
            for i, d in enumerate(z_order)
        ]
        if part > 0:
            copies.append(
                local_copy(
                    source.at[:, rows16(z), at], target.at[:, rows16(z), at], own_sem.at[0, part]
                )
            )
        return copies

    def send_xy(part):
        at = cols(*PARTS[part])
        target = early if part == 0 else near_in
        copies = [
            remote(
                near_out.at[:, rows32(spot_of(*d)), at], target.at[:, rows32(spot), at],
                xy_send.at[part, i], xy_recv.at[part, i], xy_peer(*d),
            )
            for i, d in enumerate(xy_order)
        ]
        copies.append(
            local_copy(
                near_out.at[:, rows32(spot), at], target.at[:, rows32(spot), at],
                own_sem.at[1, part],
            )
        )
        return copies

    def group_own(part):
        at = cols(*PARTS[part])
        near_out[0, :, at] = reorder(to_group, q_own[:, at]).astype(BF16)
        for t in range(2):
            near_out[t + 1, :, at] = reorder(to_group, kv_all[t, 0:ROWS, at]).astype(BF16)
        return send_xy(part)

    def group_first(copies):
        arrive(copies)
        at = cols(*PARTS[0])
        for t in range(3):
            near_out[t, :, at] = reorder(to_group, z_in[t, :, at]).astype(BF16)
        return send_xy(0)

    def spread(part, copies):
        arrive(copies)
        at = cols(*PARTS[part])
        for t in range(3):
            far_out[t, :, at] = reorder(to_frame, near_in[t, :, at]).astype(BF16)
        return send_z(part, far_out)

    half_tiles = {}

    def emit_time(tile, value):
        t_out[:, cols(tile, tile + 1)] = value.astype(BF16)

    def time_heads(part, copies):
        arrive(copies)
        if part == 0:
            at = cols(*PARTS[0])
            for t in range(3):
                home[t, :, at] = reorder(to_frame, early[t, :, at]).astype(BF16)
        heads, tiles = plan[part]
        attend_heads(heads, home.at[0], home.at[1], home.at[2], same_patch, emit_time, half_tiles)
        at = cols(*tiles)
        back = [
            remote(
                t_out.at[rows16((z + d) % 8), at], t_in.at[rows16(z), at],
                rz_send.at[part, i], rz_recv.at[part, i], z_peer(d),
            )
            for i, d in enumerate(z_order)
        ]
        back.append(
            local_copy(t_out.at[rows16(z), at], t_in.at[rows16(z), at], own_sem.at[2, part])
        )
        return back

    def group_back(part, copies):
        arrive(copies)
        at = cols(*plan[part][1])
        t_group[:, at] = reorder(to_group, t_in[:, at]).astype(BF16)
        back = [
            remote(
                t_group.at[rows32(spot_of(*d)), at], t_fin.at[rows32(spot), at],
                rxy_send.at[part, i], rxy_recv.at[part, i], xy_peer(*d),
            )
            for i, d in enumerate(xy_order)
        ]
        back.append(
            local_copy(t_group.at[rows32(spot), at], t_fin.at[rows32(spot), at], own_sem.at[3, part])
        )
        return back

    def finish(part, copies):
        arrive(copies)
        at = cols(*plan[part][1])
        out[:, at] = (acc[:, at] + reorder(to_frame, t_fin[:, at])).astype(BF16)

    def cross_attention(copies):
        arrive(copies)
        ckv[...] = jnp.zeros_like(ckv)
        for t in range(2):
            slots = jnp.concatenate([boxes[c, t].astype(F32) for c in range(8)], axis=0)
            ckv[t, 0:64, :] = slots.astype(BF16)
            first_row = lax.broadcasted_iota(jnp.int32, (16, WIDTH), 0) == 0
            null_row = jnp.broadcast_to(nulls[t : t + 1, :].astype(F32), (16, WIDTH))
            ckv[t, 64:80, :] = jnp.where(first_row, null_row, 0.0).astype(BF16)
        bv_wide[...] = jnp.zeros_like(bv_wide)
        bv_wide[:, 0:64] = bv[...]
        lane = lax.broadcasted_iota(jnp.int32, (1, ROWS), 1)
        live = ((lane < bc[...]) & (bv_wide[...] == 1)) | (lane == 64)
        cross_bias = jnp.where(live, 0.0, FAR).astype(F32)

        def emit_cross(tile, value):
            acc[:, cols(tile, tile + 1)] = value

        attend_heads(range(HEADS), cq, ckv.at[0], ckv.at[1], cross_bias, emit_cross, {})

    def emit_view(tile, value):
        at = cols(tile, tile + 1)
        acc[:, at] = acc[:, at] + value

    view_tiles = {}

    def view_heads(heads):
        linked = jnp.concatenate(
            [
                jnp.zeros((1, ROWS), F32),
                jnp.broadcast_to(jnp.where(vl[:, 0:1] == 1, 0.0, FAR).astype(F32), (1, ROWS)),
                jnp.broadcast_to(jnp.where(vl[:, 1:2] == 1, 0.0, FAR).astype(F32), (1, ROWS)),
            ],
            axis=1,
        )
        attend_heads(heads, q_own, kv_all.at[0], kv_all.at[1], linked, emit_view, view_tiles)

    odd = cam % 2
    far_peer = ((cam + 7 - 6 * odd) % 8, frame)

    def view_rows(slot):
        return pl.ds(pl.multiple_of(slot * ROWS, ROWS), ROWS)

    def send_far_view(piece):
        at = cols(*VIEW_PIECES[piece])
        return remote(
            qkv.at[pl.ds(1, 2), :, at], kv_all.at[:, view_rows(2 - odd), at],
            view_send.at[piece + 1], view_recv.at[piece + 1], far_peer,
        )

    z0 = send_z(0, qkv)
    for src, dst in (
        (qkv.at[:, rows16(z)], z_in.at[:, rows16(z)]),
        (cross_q, cq),
        (box_kv, boxes.at[cam]),
        (null_kv, nulls),
        (view_link, vl),
        (box_counts, bc),
        (box_visible, bv),
    ):
        local.append(local_copy(src, dst, local_sem.at[len(local)]))
    arrive(local[0:2])
    xy1 = group_own(1)
    xy2 = group_own(2)
    box_copies = [
        remote(box_kv, boxes.at[cam], box_send.at[i], box_recv.at[i], cam_peer(d))
        for i, d in enumerate((2, 6))
    ]
    pair_copies = [remote(box_kv, boxes.at[cam], pair_send.at[0], pair_recv.at[0], pair)]
    view_copies = [
        remote(
            qkv.at[pl.ds(1, 2)], kv_all.at[:, view_rows(1 + odd)], view_send.at[0],
            view_recv.at[0], pair,
        )
    ]
    z1 = spread(1, xy1)
    z2 = spread(2, xy2)
    xy0 = group_first(z0 + local[2:3])
    arrive(box_copies)
    for i, (d, t) in enumerate(((2, 0), (6, 1))):
        block = boxes.at[(cam + 8 - d) % 8, t]
        box_copies.append(
            remote(block, block, box_send.at[i + 2], box_recv.at[i + 2], cam_peer(d))
        )

    for piece in range(len(VIEW_PIECES)):
        view_copies.append(send_far_view(piece))
    def cross_chip(i, d):
        block = boxes.at[(cam + 8 - d) % 8]
        pair_copies.append(remote(block, block, pair_send.at[i], pair_recv.at[i], pair))

    cross_chip(1, 2)
    cross_chip(2, 6)
    r0 = time_heads(0, xy0)
    r1 = time_heads(1, z1)
    arrive(box_copies[2:4])
    cross_chip(3, 4)
    r2 = time_heads(2, z2)
    cross_attention(local[3:] + pair_copies)
    drain(z0 + xy1 + xy2 + box_copies + pair_copies)
    arrive(view_copies[0:2])
    view_heads(range(0, 5))
    f0 = group_back(0, r0)
    drain(z1 + xy0 + view_copies[0:2])
    arrive(view_copies[2:3])
    view_heads(range(5, 12))
    f1 = group_back(1, r1)
    drain(z2 + r0 + view_copies)
    drain(r1 + f0)
    f2 = group_back(2, r2)
    arrive(view_copies[3:4])
    view_heads(range(12, HEADS))
    finish(0, f0)
    finish(1, f1)
    drain(r2 + f1)
    finish(2, f2)
    drain(sent)


def in_hbm(operand):
    return pltpu.with_memory_space_constraint(operand, pltpu.HBM)


def on_device(qkv, cross_q, box_kv, null_kv, view_link, box_counts, box_visible):
    parts = len(PARTS)
    dma = pltpu.SemaphoreType.DMA
    wide = (ROWS, WIDTH)
    blended = pl.pallas_call(
        kernel,
        out_shape=jax.ShapeDtypeStruct(wide, BF16),
        in_specs=[pl.BlockSpec(memory_space=pl.ANY)] * 7,
        out_specs=pl.BlockSpec(memory_space=pltpu.VMEM),
        scratch_shapes=[
            pltpu.VMEM(wide, BF16),
            pltpu.VMEM((2, 3 * ROWS, WIDTH), BF16),
            pltpu.VMEM((3,) + wide, BF16),
            pltpu.VMEM((3,) + wide, BF16),
            pltpu.VMEM((3,) + wide, BF16),
            pltpu.VMEM((3,) + wide, BF16),
            pltpu.VMEM((3,) + wide, BF16),
            pltpu.VMEM((3,) + wide, BF16),
            pltpu.VMEM(wide, BF16),
            pltpu.VMEM(wide, BF16),
            pltpu.VMEM(wide, BF16),
            pltpu.VMEM(wide, BF16),
            pltpu.VMEM(wide, BF16),
            pltpu.VMEM((8, 2, 8, WIDTH), BF16),
            pltpu.VMEM((2, WIDTH), BF16),
            pltpu.VMEM((2,) + wide, BF16),
            pltpu.VMEM((1, 2), jnp.int32),
            pltpu.VMEM((1, 1), jnp.int32),
            pltpu.VMEM((1, 64), jnp.int32),
            pltpu.VMEM((1, 128), jnp.int32),
            pltpu.VMEM(wide, F32),
            dma((9,)),
            dma((parts, 7)),
            dma((parts, 7)),
            dma((parts, 3)),
            dma((parts, 3)),
            dma((parts, 3)),
            dma((parts, 3)),
            dma((parts, 7)),
            dma((parts, 7)),
            dma((1 + len(VIEW_PIECES),)),
            dma((1 + len(VIEW_PIECES),)),
            dma((4,)),
            dma((4,)),
            dma((4,)),
            dma((4,)),
            dma((4, parts)),
        ],
        compiler_params=pltpu.CompilerParams(
            collective_id=0, has_side_effects=True, vmem_limit_bytes=40 << 20
        ),
        name="multiview_attention",
    )(
        in_hbm(qkv[:, 0, 0]),
        in_hbm(cross_q[0, 0]),
        in_hbm(box_kv[:, 0]),
        in_hbm(null_kv),
        in_hbm(view_link),
        box_counts.reshape(1, 1),
        in_hbm(box_visible[0]),
    )
    return blended[None, None]


def solution(mesh):
    return jax.shard_map(
        on_device,
        mesh=mesh,
        in_specs=(
            P(None, "cam", "frame", None, None),
            P("cam", "frame", None, None),
            P(None, "frame", "cam", None),
            P(None, None),
            P("cam", None),
            P("frame"),
            P("cam", "frame", None),
        ),
        out_specs=P("cam", "frame", None, None),
        check_vma=False,
    )
```
